512 devices in a mesh: section: 16 (over y, core), tp: 16 (over x_lo, z), rep: 2 (over x_hi).
Axes of the slice: x: 4 (x_hi: 2, x_lo: 2; x = x_hi * 2 + x_lo), y: 8, z: 8, core: 2. Of those that a mesh axis runs over, the one named last changes fastest.
Arguments:
- student_noise: float32 [2, 3072, 64], P('rep', 'section'), may hold values from -10 to 10
- renoise_noise: float32 [2, 3072, 64], P('rep', 'section'), may hold values from -10 to 10
- patch_slot: int32 [2, 3072], P('rep', 'section'), may hold values from 0 to 3071, each once within a row
- renoise_step: int32 [2], P('rep'), may hold values from 20 to 979
- prompt_ids: int32 [2, 256], P('rep'), may hold values from 0 to 31999
- text_table: bfloat16 [32000, 2432], P(('section', 'tp')), may hold values from -48 to 48
- student_in: bfloat16 [64, 2432], replicated, may hold values from -0.75 to 0.75
- student_qkv: bfloat16 [2432, 3, 2048], P('section', None, 'tp'), may hold values from -2 to 2
- student_out: bfloat16 [2432, 2048], P('section', 'tp'), may hold values from -0.375 to 0.375
- student_final: bfloat16 [2432, 64], replicated, may hold values from -0.125 to 0.125
- real_in: bfloat16 [64, 2432], replicated, may hold values from -0.75 to 0.75
- real_qkv: bfloat16 [2432, 3, 2048], P('section', None, 'tp'), may hold values from -2 to 2
- real_out: bfloat16 [2432, 2048], P('section', 'tp'), may hold values from -0.375 to 0.375
- real_final: bfloat16 [2432, 64], replicated, may hold values from -0.125 to 0.125
- fake_in: bfloat16 [64, 2432], replicated, may hold values from -0.75 to 0.75
- fake_qkv: bfloat16 [2432, 3, 2048], P('section', None, 'tp'), may hold values from -2 to 2
- fake_out: bfloat16 [2432, 2048], P('section', 'tp'), may hold values from -0.375 to 0.375
- fake_final: bfloat16 [2432, 64], replicated, may hold values from -0.125 to 0.125
Outputs:
- latent_grad: float32 [2, 3072, 64], P('rep', 'section')
The draws below stay inside these ranges and needn't reach their ends.
All inputs are finite; a program needn't handle non-finite values. Where the reference program divides by a largest or mean magnitude, that divisor is 1e-20 or more.
Results may differ from the reference program's by a relative error of at most 0.03.
Values may be sent and summed in bfloat16 or wider, within the bound.
No kernel may reach another device: no remote copies, remote signals or barrier semaphores. Data moves between devices by JAX's collectives and lax.ppermute only.
A program may use at most 64 MiB of HBM per device.

```python
import math
import jax
import jax.numpy as jnp
from jax import lax

D = 2432
HEADS = 32
HD = 64
CH = 64
VOCAB = 32000
PROMPT = 256
GRID_W = 64
HW = 2048
TOKENS = 3072
SAMPLES = 2
N_TP = 16


def draw_student_noise(key, part):
    key = jax.random.fold_in(key, 11)
    ladder = jnp.arange(TOKENS, dtype=jnp.float32)[None, :, None] / TOKENS
    base = jnp.clip(jax.random.normal(key, (SAMPLES, TOKENS, CH), jnp.float32), -6.0, 6.0)
    return base * 0.55 * 3.0 ** ladder


def draw_renoise_noise(key, part):
    key = jax.random.fold_in(key, 23)
    ladder = jnp.arange(TOKENS, dtype=jnp.float32)[None, :, None] / TOKENS
    base = jnp.clip(jax.random.normal(key, (SAMPLES, TOKENS, CH), jnp.float32), -6.0, 6.0)
    return base * 0.55 * 3.0 ** ladder


def head_gained(pick_key, base, top):
    order = jax.random.permutation(pick_key, HEADS)
    rank = order.astype(jnp.float32) / (HEADS - 1)
    gains = jnp.float32(top) ** rank
    columns = jnp.repeat(gains, HD)
    factor = jnp.stack([columns, columns, jnp.ones((HEADS * HD,), jnp.float32)])
    return jnp.clip(base * factor[None, :, :] * D ** (-0.5), -2.0, 2.0)


def draw_student_qkv(key, part):
    key = jax.random.fold_in(key, 31)
    base_key, pick_key = jax.random.split(key)
    base = jnp.clip(jax.random.normal(base_key, (D, 3, HEADS * HD), jnp.float32), -6.0, 6.0)
    return head_gained(pick_key, base, 2.5).astype(jnp.bfloat16)


def draw_real_qkv(key, part):
    key = jax.random.fold_in(key, 37)
    base_key, pick_key = jax.random.split(key)
    base = jnp.clip(jax.random.normal(base_key, (D, 3, HEADS * HD), jnp.float32), -6.0, 6.0)
    return head_gained(pick_key, base, 2.5).astype(jnp.bfloat16)


def draw_fake_qkv(key, part):
    key = jax.random.fold_in(key, 41)
    base_key, pick_key = jax.random.split(key)
    base = jnp.clip(jax.random.normal(base_key, (D, 3, HEADS * HD), jnp.float32), -6.0, 6.0)
    return head_gained(pick_key, base, 2.5).astype(jnp.bfloat16)


def set_ends(drawn, rng, smallest, largest):
    index_at = [jax.random.randint(jax.random.fold_in(rng, axis), (), 0, length) for axis, length in enumerate(drawn.shape)]
    main_axis = drawn.shape.index(max(drawn.shape))
    beside = index_at[:main_axis] + [(index_at[main_axis] + 1) % drawn.shape[main_axis]] + index_at[main_axis + 1:]
    return drawn.at[tuple(index_at)].set(smallest).at[tuple(beside)].set(largest)


def levels(rng, shape, cuts, smallest, top_value):
    gain, own = 1.0, jax.random.fold_in(rng, 6)
    for axis_at, blocks in cuts:
        heights = jnp.exp(jax.random.uniform(jax.random.fold_in(own, axis_at), (blocks,), jnp.float32, smallest / len(cuts), top_value / len(cuts)))
        gain = gain * jnp.repeat(heights, shape[axis_at] // blocks).reshape([-1 if axis == axis_at else 1 for axis in range(len(shape))])
    return gain


def centred(own_key, shape, deviation, limit, shards=(), kind=jnp.bfloat16):
    gain = levels(own_key, shape, shards, -0.22, 0.18) if shards else 1.0
    drawn = jax.random.normal(own_key, shape, jnp.float32) * deviation * gain
    return jnp.minimum(jnp.maximum(drawn, -limit), limit).astype(kind)


def setup_inputs(seed: int = 0) -> dict:
    seeds = jax.random.split(jax.random.key(seed), 19)
    student_noise = draw_student_noise(jax.random.fold_in(seeds[18], 71), 0)
    renoise_noise = draw_renoise_noise(jax.random.fold_in(seeds[18], 71), 0)
    patch_slot = jax.vmap(lambda own: jax.random.permutation(own, TOKENS))(jax.random.split(seeds[2], SAMPLES)).reshape((SAMPLES, TOKENS)).astype(jnp.int32)
    renoise_step = jax.random.randint(seeds[3], (SAMPLES,), 20, 980).astype(jnp.int32)
    prompt_ids = set_ends(jax.random.randint(seeds[4], (SAMPLES, PROMPT), 0, VOCAB), jax.random.fold_in(seeds[4], 1), 0, VOCAB - 1).astype(jnp.int32)
    text_table = centred(seeds[5], (VOCAB, D), 8.0, 48.0, ((0, 256),))
    student_in = centred(seeds[6], (CH, D), CH ** -0.5, 0.75)
    student_qkv = draw_student_qkv(jax.random.fold_in(seeds[18], 71), 0)
    student_out = centred(seeds[8], (D, HW), (HW // 9) ** -0.5, 0.375, ((0, 16), (1, 16)))
    student_final = centred(seeds[9], (D, CH), D ** -0.5, 0.125)
    real_in = centred(seeds[10], (CH, D), CH ** -0.5, 0.75)
    real_qkv = draw_real_qkv(jax.random.fold_in(seeds[18], 71), 0)
    real_out = centred(seeds[12], (D, HW), (HW // 9) ** -0.5, 0.375, ((0, 16), (1, 16)))
    real_final = centred(seeds[13], (D, CH), D ** -0.5, 0.125)
    fake_in = centred(seeds[14], (CH, D), CH ** -0.5, 0.75)
    fake_qkv = draw_fake_qkv(jax.random.fold_in(seeds[18], 71), 0)
    fake_out = centred(seeds[16], (D, HW), (HW // 9) ** -0.5, 0.375, ((0, 16), (1, 16)))
    fake_final = centred(seeds[17], (D, CH), D ** -0.5, 0.125)
    return dict(student_noise=student_noise, renoise_noise=renoise_noise, patch_slot=patch_slot, renoise_step=renoise_step, prompt_ids=prompt_ids, text_table=text_table, student_in=student_in, student_qkv=student_qkv, student_out=student_out, student_final=student_final, real_in=real_in, real_qkv=real_qkv, real_out=real_out, real_final=real_final, fake_in=fake_in, fake_qkv=fake_qkv, fake_out=fake_out, fake_final=fake_final)


def time_embed(step_time):
    half_width = D // 2
    frequency = jnp.exp(-math.log(10000.0) * jnp.arange(half_width, dtype=jnp.float32) / half_width)
    angles = 1000.0 * step_time * frequency
    return jnp.concatenate([jnp.cos(angles), jnp.sin(angles)])

def place_embed(slots):
    quarter = D // 4
    frequency = jnp.exp(-math.log(10000.0) * jnp.arange(quarter, dtype=jnp.float32) / quarter)
    row_angle = (slots // GRID_W).astype(jnp.float32)[:, None] * frequency[None, :]
    col_angle = (slots % GRID_W).astype(jnp.float32)[:, None] * frequency[None, :]
    return jnp.concatenate([jnp.sin(row_angle), jnp.cos(row_angle), jnp.sin(col_angle), jnp.cos(col_angle)], axis=1)

def rms_norm(values):
    return values * lax.rsqrt(lax.optimization_barrier(jnp.mean(values * values, axis=-1, keepdims=True)) + 1e-06)

def attend_head(triple):
    query_head, key_head, value_head = triple
    scores = jnp.dot(query_head, key_head.T, preferred_element_type=jnp.float32) * HD ** (-0.5)
    row_max = lax.optimization_barrier(jnp.max(scores, axis=1, keepdims=True))
    expo = jnp.exp(scores - row_max)
    totals = lax.optimization_barrier(jnp.sum(expo, axis=1, keepdims=True))
    mixed = jnp.dot(expo.astype(jnp.bfloat16), value_head, preferred_element_type=jnp.float32) / totals
    return mixed.astype(jnp.bfloat16)

def network(latent, step_time, condition, w_in, w_qkv, w_out, w_final):
    hidden = jnp.dot(latent.astype(jnp.bfloat16), w_in, preferred_element_type=jnp.float32)
    hidden = hidden + condition + time_embed(step_time)[None, :]
    normed = rms_norm(hidden).astype(jnp.bfloat16)
    projected = jnp.einsum('td,dkc->tkc', normed.astype(jnp.float32), w_qkv.astype(jnp.float32)).astype(jnp.bfloat16)
    heads_query = projected[:, 0].reshape(TOKENS, HEADS, HD).transpose(1, 0, 2)
    heads_key = projected[:, 1].reshape(TOKENS, HEADS, HD).transpose(1, 0, 2)
    heads_value = projected[:, 2].reshape(TOKENS, HEADS, HD).transpose(1, 0, 2)
    mixed = lax.map(attend_head, (heads_query, heads_key, heads_value))
    mixed = mixed.transpose(1, 0, 2).reshape(TOKENS, HEADS * HD)
    group_width = HEADS * HD // N_TP

    def add_group(running, group_index):
        part_mixed = lax.dynamic_slice_in_dim(mixed, group_index * group_width, group_width, 1)
        part_weight = lax.dynamic_slice_in_dim(w_out, group_index * group_width, group_width, 1)
        group_term = jnp.dot(part_mixed, part_weight.T, preferred_element_type=jnp.float32).astype(jnp.bfloat16)
        group_term = lax.optimization_barrier(group_term).astype(jnp.float32)
        return (running + group_term, group_index)
    attended, unused = lax.scan(add_group, jnp.zeros((TOKENS, D), jnp.float32), jnp.arange(N_TP, dtype=jnp.int32))
    after = hidden + attended
    return jnp.dot(rms_norm(after).astype(jnp.bfloat16), w_final, preferred_element_type=jnp.float32)

def reference(student_noise, renoise_noise, patch_slot, renoise_step, prompt_ids, text_table, student_in, student_qkv, student_out, student_final, real_in, real_qkv, real_out, real_final, fake_in, fake_qkv, fake_out, fake_final):
    results = []
    for sample in range(SAMPLES):
        pooled = lax.optimization_barrier(jnp.mean(text_table[prompt_ids[sample]].astype(jnp.float32), axis=0))
        condition = place_embed(patch_slot[sample]) + pooled[None, :]
        start_noise = student_noise[sample]
        velocity = network(start_noise, jnp.float32(1.0), condition, student_in, student_qkv, student_out, student_final)
        clean = start_noise - velocity
        step_time = renoise_step[sample].astype(jnp.float32) / 1000.0
        noisy = (1.0 - step_time) * clean + step_time * renoise_noise[sample]
        real_velocity = network(noisy, step_time, condition, real_in, real_qkv, real_out, real_final)
        fake_velocity = network(noisy, step_time, condition, fake_in, fake_qkv, fake_out, fake_final)
        pred_real = noisy - step_time * real_velocity
        pred_fake = noisy - step_time * fake_velocity
        spread = jnp.mean(jnp.abs(clean - pred_real)) + 1e-05
        results.append((pred_fake - pred_real) / spread)
    return jnp.stack(results)
```

```python
import math

import jax
import jax.numpy as jnp
import numpy as np
from jax import lax
from jax.experimental import pallas as pl
from jax.experimental.pallas import tpu as pltpu
from jax.sharding import Mesh, PartitionSpec as P

D = 2432
HD = 64
GRID_W = 64
GRID_H = 48
CH = 64
BASIS = 192
ROW0, ONE, COL0 = 64, 112, 128
EPS = 1e-06
SEC = ("y", "core")
TP = ("xl", "zh", "zp")
N_SEC = 16
PROMPT = 256
N_TP = 16
LOCAL = 192
OWN = 12
TOKENS = 3072
KEYS = 1536
QUART = D // 4
SLOTS, SHARES, MESSAGE = 96, 104, 144
VMEM = 60 * 2**20
bf16 = jnp.bfloat16
f32 = jnp.float32


def nn(a, b):
    return jnp.dot(a, b, preferred_element_type=f32)


def nt(a, b):
    return lax.dot_general(a, b, (((1,), (1,)), ((), ())), preferred_element_type=f32)


def split2(values):
    high = values.astype(bf16)
    return high, (values - high.astype(f32)).astype(bf16)


def features(message):
    z = message[:SLOTS]
    z = jnp.concatenate([z, jnp.concatenate([z[:, CH:], z[:, :CH]], axis=1)], axis=0)
    slots = message[SLOTS:SHARES].astype(f32).T
    row = jnp.concatenate([slots[:, 0:1], slots[:64, 1:2]], axis=0)
    col = jnp.concatenate([slots[:, 2:3], slots[:64, 3:4]], axis=0)
    lane = lax.broadcasted_iota(jnp.int32, (LOCAL, 128), 1).astype(f32)
    rest = ((lane == row + ROW0) | (lane == ONE)).astype(f32).astype(bf16)
    hot = (lane[:, :GRID_W] == col).astype(f32).astype(bf16)
    return z, rest, hot


def own_tokens(g):
    row = lax.broadcasted_iota(jnp.int32, (OWN, LOCAL), 0)
    col = lax.broadcasted_iota(jnp.int32, (OWN, LOCAL), 1)
    return (col == row * N_TP + g).astype(f32)


def prepare_kernel(high_ref, low_ref, w1_ref, w2_ref, w3_ref, time_ref, shares_ref, hid_high_ref, hid_low_ref, gram_ref):
    pooled = shares_ref[0]
    for g in range(1, N_TP):
        pooled = pooled + shares_ref[g]
    pooled = pooled / PROMPT
    pooled = jnp.concatenate([pooled[k : k + 1] for k in range(D // 128)], axis=1)
    is_one = lax.broadcasted_iota(jnp.int32, (16, D), 0) == 0
    for net, w_ref in enumerate((w1_ref, w2_ref, w3_ref)):
        bias = jnp.broadcast_to(time_ref[net : net + 1, :] + pooled, (16, D))
        bias = jnp.where(is_one, bias, 0.0)
        for ref, table_ref, part in zip((hid_high_ref, hid_low_ref), (high_ref, low_ref), split2(bias)):
            ref[net, :CH, :] = w_ref[...] if ref is hid_high_ref else jnp.zeros((CH, D), bf16)
            ref[net, ROW0:ONE, :] = table_ref[:GRID_H]
            ref[net, ONE:COL0, :] = part
            ref[net, COL0:, :] = table_ref[GRID_H:]
        high, low = hid_high_ref[net], hid_low_ref[net]
        cross = nt(high, low)
        gram_ref[net] = nt(high, high) + cross + nt(low, high)


def project_kernel(pick_ref, hid_ref, w_ref, out_ref):
    out_ref[0] = nn(hid_ref[0], w_ref[0]).astype(bf16)


def project(pick, hid, w):
    return pl.pallas_call(
        project_kernel,
        grid_spec=pltpu.PrefetchScalarGridSpec(
            num_scalar_prefetch=1,
            grid=(3,),
            in_specs=[
                pl.BlockSpec((1, BASIS, D), lambda k, pick: (pick[1], 0, 0)),
                pl.BlockSpec((1, D, 128), lambda k, pick: (pick[0] + k, 0, 0)),
            ],
            out_specs=pl.BlockSpec((1, BASIS, 128), lambda k, pick: (k, 0, 0)),
        ),
        out_shape=jax.ShapeDtypeStruct((3, BASIS, 128), bf16),
        compiler_params=pltpu.CompilerParams(vmem_limit_bytes=VMEM),
        cost_estimate=pl.CostEstimate(flops=2 * BASIS * D * 384, bytes_accessed=3 * 10**6, transcendentals=0),
        name="project",
    )(pick, hid, w)


def attend_kernel(nets, members, packed, wout_at, place_ref, base_ref, *refs):
    if packed:
        z_ref, *refs = refs
    gram_ref, *refs = refs
    proj_refs = refs[:-9]
    wout_hbm, out_ref, x_ref, qp_ref, s_ref, sc_ref, wout_ref, z32_ref, sem = refs[-9:]
    s, xl, zh, core = place_ref[0], place_ref[2], place_ref[3], place_ref[4]
    shares = N_TP // members
    count = shares * OWN
    load = pltpu.make_async_copy(wout_hbm.at[pl.ds(wout_at, members * nets)], wout_ref, sem)
    load.start()
    if packed:
        z32_ref[...] = z_ref[...].astype(f32)
        for sec in range(N_SEC):
            unused, rest, hot = features(base_ref[sec])
            for j in range(OWN):
                at = (j * N_SEC + sec) * 16
                x_ref[at : at + 16, :128] = rest[j * 16 : (j + 1) * 16]
                x_ref[at : at + 16, COL0:] = hot[j * 16 : (j + 1) * 16]
        lane = lax.broadcasted_iota(jnp.int32, (256, 128), 1)
        for j in range(OWN):
            chunk = z32_ref[pl.ds(j // 2, 256, stride=8), :].astype(bf16)
            if j % 2:
                chunk = jnp.concatenate([chunk[:, 64:], chunk[:, :64]], axis=1)
            at = slice(j * 256, (j + 1) * 256)
            x_ref[at, :128] = jnp.where(lane < CH, chunk, x_ref[at, :128])
        own = jnp.concatenate(
            [x_ref[pl.ds(pl.multiple_of((j * N_SEC + s) * 16, 16), 16), :] for j in range(OWN)], axis=0
        )
        scales = z32_ref[pl.ds(6, 256, stride=8), :].T
        for net in range(nets):
            for j in range(OWN):
                line = net * 32 + j
                line = scales[line : line + 1] + scales[line + 16 : line + 17]
                at = j * 256
                sc_ref[net, at // KEYS, :, at % KEYS : at % KEYS + 256] = jnp.broadcast_to(line, (8, 256))
    else:
        for sec in range(N_SEC):
            z, rest, hot = features(base_ref[sec])
            lane = lax.broadcasted_iota(jnp.int32, z.shape, 1)
            x_ref[sec * LOCAL : (sec + 1) * LOCAL, :128] = jnp.where(lane < CH, z, rest)
            x_ref[sec * LOCAL : (sec + 1) * LOCAL, COL0:] = hot
        own = x_ref[pl.ds(pl.multiple_of(s * LOCAL, LOCAL), LOCAL), :]
    row = lax.broadcasted_iota(jnp.int32, (count, LOCAL), 0)
    col = lax.broadcasted_iota(jnp.int32, (count, LOCAL), 1)
    share = lax.shift_right_logical(row * 171, 11)
    if members == 2:
        owner = xl * 8 + share
    else:
        owner = lax.shift_right_logical(share, 1) * 8 + zh * 2 + lax.bitwise_and(share, 1)
    order = (col == (row - share * OWN) * N_TP + owner).astype(bf16)
    queries = nn(order, own).astype(bf16)
    eye = (
        lax.broadcasted_iota(jnp.int32, (BASIS, BASIS), 0) == lax.broadcasted_iota(jnp.int32, (BASIS, BASIS), 1)
    ).astype(bf16)
    heads = [(member, slice(half * HD, (half + 1) * HD)) for member in range(members) for half in range(2)]
    rows = len(heads) * count
    for turn in range(nets):
        net = lax.bitwise_xor(core, turn) if nets == 2 else 0
        gram_high, gram_low = split2(gram_ref[net])
        energy = jnp.sum(
            (nn(queries, gram_high) + nn(queries, gram_low)) * queries.astype(f32), axis=1, keepdims=True
        )
        scale = lax.rsqrt(energy / D + EPS)

        def proj(member, kind):
            if nets == 2:
                return proj_refs[turn][member, kind]
            return proj_refs[member][kind]

        for h, (member, part) in enumerate(heads):
            if part.start == 0:
                q = (nn(queries, proj(member, 0)) * scale).astype(bf16)
            qp_ref[h * count : (h + 1) * count, :] = (
                nt(q[:, part], proj(member, 1)[:, part]) * HD ** (-0.5)
            ).astype(bf16)

        def score(block, top):
            keys = x_ref[pl.ds(pl.multiple_of(block * KEYS, KEYS), KEYS), :]
            if not packed:
                energy = (nt(gram_high, keys) + nt(gram_low, keys)) * nt(eye, keys)
                scale = lax.rsqrt(jnp.sum(energy, axis=0, keepdims=True) / D + EPS)
                sc_ref[net, block] = jnp.broadcast_to(scale, (8, KEYS))
            scores = nt(qp_ref[...], keys) * sc_ref[net, block][:1]
            s_ref[block] = scores
            for part in range(KEYS // 128):
                top = jnp.maximum(top, scores[:, part * 128 : (part + 1) * 128])
            return top

        top = lax.fori_loop(0, TOKENS // KEYS, score, jnp.full((rows, 128), -1e30, f32))
        top = jnp.max(top, axis=1, keepdims=True)

        def mix(block, carry):
            total, mixed = carry
            expo = jnp.exp(s_ref[block] - top)
            for part in range(KEYS // 128):
                total = total + expo[:, part * 128 : (part + 1) * 128]
            weights = (expo * sc_ref[net, block][:1]).astype(bf16)
            keys = x_ref[pl.ds(pl.multiple_of(block * KEYS, KEYS), KEYS), :]
            return total, mixed + nn(weights, keys)

        total, mixed = lax.fori_loop(
            0, TOKENS // KEYS, mix, (jnp.zeros((rows, 128), f32), jnp.zeros((rows, BASIS), f32))
        )
        mixed = (mixed / jnp.sum(total, axis=1, keepdims=True)).astype(bf16)
        if turn == 0:
            load.wait()
        values = [
            nn(mixed[h * count : (h + 1) * count], proj(member, 2)[:, part]) for h, (member, part) in enumerate(heads)
        ]
        values = jnp.concatenate(values, axis=1).astype(bf16)
        term = []
        for part in range(4):
            at = slice(part * QUART, (part + 1) * QUART)
            term.append(nt(values, jnp.concatenate([wout_ref[m * nets + net, at, :] for m in range(members)], axis=1)))
        for d in range(shares):
            block = jnp.concatenate([t[d * OWN : (d + 1) * OWN] for t in term], axis=0).astype(bf16)
            if nets == 2:
                out_ref[d, pl.ds(pl.multiple_of(net * 48, 16), 48), :] = block
            else:
                out_ref[d] = block


def attend(place, base, z, gram_at, gram, proj, wout_at, wout):
    nets = 1 if z is None else 2
    members = 2 if z is None else 4
    packed = z is not None
    args = (base, z) if packed else (base,)
    rows = 2 * members * OWN * (N_TP // members)
    whole = lambda a: pl.BlockSpec(a.shape, lambda i: (0,) * a.ndim)
    out = jax.ShapeDtypeStruct((N_TP // members, nets * 4 * OWN, QUART), bf16)
    return pl.pallas_call(
        lambda *refs: attend_kernel(nets, members, packed, wout_at, *refs),
        out_shape=out,
        grid=(1,),
        in_specs=[pl.BlockSpec(memory_space=pltpu.SMEM)]
        + [whole(a) for a in args]
        + [pl.BlockSpec((nets, BASIS, BASIS), lambda i: (gram_at, 0, 0))]
        + [whole(a) for a in proj]
        + [pl.BlockSpec(memory_space=pl.ANY)],
        out_specs=whole(out),
        scratch_shapes=[
            pltpu.VMEM((TOKENS, BASIS), bf16),
            pltpu.VMEM((rows, BASIS), bf16),
            pltpu.VMEM((TOKENS // KEYS, rows, KEYS), f32),
            pltpu.VMEM((nets, TOKENS // KEYS, 8, KEYS), f32),
            pltpu.VMEM((members * nets, D, 128), bf16),
            pltpu.VMEM((N_SEC * N_TP * 8, 128), f32),
            pltpu.SemaphoreType.DMA,
        ],
        compiler_params=pltpu.CompilerParams(vmem_limit_bytes=VMEM),
        cost_estimate=pl.CostEstimate(flops=nets * 4 * 10**9, bytes_accessed=10**7, transcendentals=nets * 1200000),
        name="attend",
    )(place, *args, gram, *proj, wout)


def finish(recv_ref, net, hidden, w_final):
    rows = slice(net * 4 * OWN, (net + 1) * 4 * OWN)
    terms = recv_ref[0, rows].astype(f32)
    for d in range(1, recv_ref.shape[0]):
        terms = terms + recv_ref[d, rows].astype(f32)
    afters = []
    energy = jnp.zeros((OWN, 1), f32)
    for part in range(4):
        after = hidden[:, part * QUART : (part + 1) * QUART] + terms[part * OWN : (part + 1) * OWN]
        energy = energy + jnp.sum(after * after, axis=1, keepdims=True)
        afters.append(after)
    scale = lax.rsqrt(energy / D + EPS)
    normed = jnp.concatenate([after * scale for after in afters], axis=1).astype(bf16)
    return nt(normed, w_final[...])


def own_kernel(place_ref, message_ref, high_ref, low_ref, x12_ref, hidden_ref):
    z, rest, hot = features(message_ref[...])
    lane = lax.broadcasted_iota(jnp.int32, z.shape, 1)
    full = jnp.concatenate([jnp.where(lane < CH, z, rest), hot], axis=1)
    x12 = nn(own_tokens(place_ref[1]).astype(bf16), full).astype(bf16)
    x12_ref[...] = x12
    hidden_ref[...] = nn(x12, high_ref[0]) + nn(x12, low_ref[0])


def scores_own_kernel(after_ref, x12_ref, high_ref, low_ref, hidden_ref):
    for net in range(2):
        hidden_ref[net] = nn(x12_ref[...], high_ref[net]) + nn(x12_ref[...], low_ref[net])


def student_kernel(
    place_ref, time_ref, recv_ref, hidden_ref, own12_ref, noise_ref, renoise_ref, wf_ref, gram_ref,
    x0_ref, noisy_ref, x12_ref, send_ref,
):
    pick = own_tokens(place_ref[1])
    x12 = own12_ref[...]
    velocity = finish(recv_ref, 0, hidden_ref[...], wf_ref)
    exact = lax.Precision.HIGHEST
    noise = jnp.dot(pick, noise_ref[...], precision=exact, preferred_element_type=f32)
    renoise = jnp.dot(pick, renoise_ref[...], precision=exact, preferred_element_type=f32)
    x0 = noise - velocity
    t = time_ref[0]
    noisy = (1.0 - t) * x0 + t * renoise
    x12 = jnp.concatenate([noisy.astype(bf16), x12[:, CH:]], axis=1)
    x0_ref[...] = x0
    noisy_ref[...] = noisy
    x12_ref[...] = x12
    row = lax.broadcasted_iota(jnp.int32, (OWN, 128), 0)
    lane = lax.broadcasted_iota(jnp.int32, (OWN, 128), 1)
    scales = jnp.zeros((OWN, 128), f32)
    for net in range(2):
        high, low = split2(gram_ref[net])
        energy = jnp.sum((nn(x12, high) + nn(x12, low)) * x12.astype(f32), axis=1, keepdims=True)
        for part, value in enumerate(split2(lax.rsqrt(energy / D + EPS))):
            scales = jnp.where(lane == row + (net * 32 + part * 16), value.astype(f32), scales)
    scales = jnp.sum(scales, axis=0, keepdims=True)
    pairs = [jnp.concatenate([noisy[j : j + 1], noisy[j + 1 : j + 2]], axis=1) for j in range(0, OWN, 2)]
    send_ref[...] = jnp.concatenate(pairs + [scales, jnp.zeros((1, 128), f32)], axis=0).astype(bf16)


def score_kernel(
    time_ref, recv_ref, x0_ref, noisy_ref, hidden_ref, wr_ref, wf_ref, send_ref
):
    noisy = noisy_ref[...]
    real = finish(recv_ref, 0, hidden_ref[0], wr_ref)
    fake = finish(recv_ref, 1, hidden_ref[1], wf_ref)
    t = time_ref[0]
    gap = jnp.abs(x0_ref[...] - (noisy - t * real))
    gap = jnp.sum(jnp.sum(gap, axis=1, keepdims=True), axis=0, keepdims=True)
    grad = t * (real - fake)
    packed = [jnp.concatenate([grad[j : j + 1], grad[j + 1 : j + 2]], axis=1) for j in range(0, OWN, 2)]
    packed = jnp.concatenate([*packed, jnp.broadcast_to(gap, (1, 128)), jnp.zeros((1, 128), f32)], axis=0)
    send_ref[...] = jnp.broadcast_to(packed[None], send_ref.shape)


def call(kernel, shapes, smem, *args):
    def spec(arg):
        if isinstance(arg, tuple):
            array, n, at = arg
            return pl.BlockSpec((n, *array.shape[1:]), lambda i: (at,) + (0,) * (array.ndim - 1))
        return pl.BlockSpec(arg.shape, lambda i: (0,) * len(arg.shape))

    return pl.pallas_call(
        kernel,
        out_shape=shapes,
        grid=(1,),
        in_specs=[pl.BlockSpec(memory_space=pltpu.SMEM)] * smem + [spec(arg) for arg in args[smem:]],
        out_specs=jax.tree.map(spec, shapes),
        compiler_params=pltpu.CompilerParams(vmem_limit_bytes=VMEM),
        cost_estimate=pl.CostEstimate(flops=10**9, bytes_accessed=10**7, transcendentals=0),
        name=kernel.__name__,
    )(*[arg[0] if isinstance(arg, tuple) else arg for arg in args])


def swap(values, axes):
    return lax.all_to_all(values, axes, 0, 0, tiled=False)


def spread_to(values, axes, count):
    return swap(jnp.broadcast_to(values[None], (count, *values.shape)), axes)


def shift(values, axis, count, step):
    return lax.ppermute(values, axis, [((i + step) % count, i) for i in range(count)])


def place_tables():
    quarter = D // 4
    frequency = np.exp(-math.log(10000.0) * np.arange(quarter, dtype=np.float64) / quarter)
    table = np.zeros((GRID_H + GRID_W, D), np.float32)
    row = np.arange(GRID_H)[:, None] * frequency[None, :]
    col = np.arange(GRID_W)[:, None] * frequency[None, :]
    table[:GRID_H, : D // 2] = np.concatenate([np.sin(row), np.cos(row)], axis=1)
    table[GRID_H:, D // 2 :] = np.concatenate([np.sin(col), np.cos(col)], axis=1)
    high = table.astype(bf16)
    return jnp.asarray(high), jnp.asarray((table - high.astype(np.float32)).astype(bf16))


def time_embed(step_time):
    half_width = D // 2
    frequency = jnp.exp(-math.log(10000.0) * jnp.arange(half_width, dtype=f32) / half_width)
    angles = 1000.0 * step_time * frequency
    return jnp.concatenate([jnp.cos(angles), jnp.sin(angles)])


def per_device(
    student_noise,
    renoise_noise,
    patch_slot,
    renoise_step,
    prompt_ids,
    text_table,
    student_in,
    student_qkv,
    student_out,
    student_final,
    real_in,
    real_qkv,
    real_out,
    real_final,
    fake_in,
    fake_qkv,
    fake_out,
    fake_final,
):
    s = lax.axis_index(SEC)
    g = lax.axis_index(TP)
    core = lax.axis_index("core")
    place = jnp.stack([s, g, lax.axis_index("xl"), lax.axis_index("zh"), core]).astype(jnp.int32)
    step_time = renoise_step[0].astype(f32) / 1000.0

    vocab_local = text_table.shape[0]
    first_row = (s * N_TP + g) * vocab_local
    prompt_row = prompt_ids[0] - first_row
    matches = (prompt_row[:, None] == jnp.arange(vocab_local, dtype=jnp.int32)[None, :]).astype(f32)
    counts = jnp.sum(matches, axis=0).astype(bf16)
    partial_pool = nn(counts[None], text_table).reshape(D // 128, 128)
    noise = student_noise[0]
    packed = noise.astype(bf16)
    packed = jnp.concatenate([packed[:SLOTS], packed[SLOTS:]], axis=1)
    slot = patch_slot[0]
    lines = jnp.stack([slot // GRID_W, slot % GRID_W]).astype(bf16)
    lines = jnp.pad(jnp.pad(lines, ((0, 0), (0, 64))).reshape(4, 128), ((0, 4), (0, 0)))
    own = jnp.concatenate([packed, lines, *split2(partial_pool), jnp.zeros((2, 128), bf16)], axis=0)
    out_peer = shift(student_out, "xl", 2, 1)[None]
    out_peer, own = lax.optimization_barrier((out_peer, own))
    base = spread_to(own, SEC, N_SEC)
    out2 = jnp.stack([real_out, fake_out])
    out2, own = lax.optimization_barrier((out2, own))
    out2 = lax.all_gather(out2, "zh", axis=0, tiled=True)
    shares = base[:, SHARES : SHARES + 38].astype(f32).reshape(N_SEC * 2, D // 128, 128)
    shares = jnp.sum(shares, axis=0)
    shares, out2 = lax.optimization_barrier((shares, out2))
    shares = spread_to(shares, TP, N_TP)

    def columns(qkv):
        return jnp.transpose(qkv, (1, 0, 2))

    def gather(*parts):
        return lax.all_gather(jnp.concatenate(parts, axis=0), SEC, axis=1, tiled=True)

    first = gather(columns(student_qkv), columns(real_qkv), columns(fake_qkv), student_out[None], out_peer)

    one = jax.ShapeDtypeStruct
    times = jnp.stack([time_embed(t) for t in (step_time, step_time, jnp.float32(1.0))])
    high, low, gram = call(
        prepare_kernel,
        (one((3, BASIS, D), bf16), one((3, BASIS, D), bf16), one((3, BASIS, BASIS), f32)),
        0,
        *place_tables(),
        real_in,
        fake_in,
        student_in,
        times,
        shares,
    )
    first, gram = lax.optimization_barrier((first, gram))
    out2, first = lax.optimization_barrier((out2, first))
    wout2 = gather(out2)
    zero = jnp.int32(0)
    proj1 = project(jnp.stack([zero, zero + 2]), high, first)
    peer1 = shift(proj1, "xl", 2, 1)
    pick = jnp.stack([3 + 3 * core, core])
    pick, place, proj1 = lax.optimization_barrier((pick, place, proj1))
    proj2 = project(pick, high, first)
    x12, hidden = call(
        own_kernel, (one((OWN, BASIS), bf16), one((OWN, D), f32)), 1, place, own, (high, 1, 2), (low, 1, 2)
    )
    proj2, hidden, place = lax.optimization_barrier((proj2, hidden, place))
    terms = attend(place, base, None, 2, gram, (proj1, peer1), 9, first)
    terms = swap(terms, ("zh", "zp"))
    x0, noisy, x12, message = call(
        student_kernel,
        (one((OWN, CH), f32), one((OWN, CH), f32), one((OWN, BASIS), bf16), one((8, 128), bf16)),
        2,
        place,
        step_time[None],
        terms,
        hidden,
        x12,
        noise,
        renoise_noise[0],
        student_final.T,
        (gram, 2, 0),
    )
    proj2, message = lax.optimization_barrier((proj2, message))
    proj2 = lax.all_gather(proj2, "zh", axis=0, tiled=False)
    everyone = spread_to(message, SEC + TP, N_SEC * N_TP).reshape(N_SEC * N_TP * 8, 128)
    proj2 = (proj2, shift(proj2, "core", 2, 1))
    terms = attend(place, base, everyone, 0, gram, proj2, 0, wout2)
    x12, terms = lax.optimization_barrier((x12, terms))
    hidden = call(
        scores_own_kernel, one((2, OWN, D), f32), 1, place, x12, (high, 2, 0), (low, 2, 0)
    )
    terms = swap(terms, ("xl", "zp"))
    message = call(
        score_kernel,
        one((N_TP, 8, 128), f32),
        1,
        step_time[None],
        terms,
        x0,
        noisy,
        hidden,
        real_final.T,
        fake_final.T,
    )
    near = swap(message, TP)
    gap = spread_to(jnp.sum(near[:, 6:7], axis=0), SEC, N_SEC)
    spread = jnp.sum(gap[:, 0, 0]) / (TOKENS * CH) + 1e-05
    grad = jnp.transpose(near[:, :6].reshape(N_TP, 6, 2, CH), (1, 2, 0, 3))
    return (grad.reshape(LOCAL, CH) / spread)[None]


def solution(mesh):
    fine = Mesh(mesh.devices.reshape(8, 2, 2, 4, 2, 2), ("y", "core", "xl", "zh", "zp", "rep"))
    qkv = P(SEC, None, TP)
    out = P(SEC, TP)
    net = (P(), qkv, out, P())
    placed = (
        P("rep", SEC, None),
        P("rep", SEC, None),
        P("rep", SEC),
        P("rep"),
        P("rep", None),
        P(SEC + TP, None),
    ) + net * 3
    return jax.shard_map(
        per_device, mesh=fine, in_specs=placed, out_specs=P("rep", SEC, None), check_vma=False
    )
```

```python
import math

import jax
import jax.numpy as jnp
import numpy as np
from jax import lax
from jax.experimental import pallas as pl
from jax.experimental.pallas import tpu as pltpu
from jax.sharding import Mesh, PartitionSpec as P

D = 2432
HD = 64
GRID_W = 64
GRID_H = 48
CH = 64
BASIS = 192
ROW0, ONE, COL0 = 64, 112, 128
EPS = 1e-06
SEC = ("y", "core")
TP = ("xl", "zh", "zp")
N_SEC = 16
PROMPT = 256
N_TP = 16
LOCAL = 192
OWN = 12
TOKENS = 3072
KEYS = 1536
QUART = D // 4
SLOTS, SHARES, MESSAGE = 96, 104, 144
VMEM = 60 * 2**20
bf16 = jnp.bfloat16
f32 = jnp.float32


def nn(a, b):
    return jnp.dot(a, b, preferred_element_type=f32)


def nt(a, b):
    return lax.dot_general(a, b, (((1,), (1,)), ((), ())), preferred_element_type=f32)


def split2(values):
    high = values.astype(bf16)
    return high, (values - high.astype(f32)).astype(bf16)


def features(message):
    z = message[:SLOTS]
    z = jnp.concatenate([z, jnp.concatenate([z[:, CH:], z[:, :CH]], axis=1)], axis=0)
    slots = message[SLOTS:SHARES].astype(f32).T
    row = jnp.concatenate([slots[:, 0:1], slots[:64, 1:2]], axis=0)
    col = jnp.concatenate([slots[:, 2:3], slots[:64, 3:4]], axis=0)
    lane = lax.broadcasted_iota(jnp.int32, (LOCAL, 128), 1).astype(f32)
    rest = ((lane == row + ROW0) | (lane == ONE)).astype(f32).astype(bf16)
    hot = (lane[:, :GRID_W] == col).astype(f32).astype(bf16)
    return z, rest, hot


def own_tokens(g):
    row = lax.broadcasted_iota(jnp.int32, (OWN, LOCAL), 0)
    col = lax.broadcasted_iota(jnp.int32, (OWN, LOCAL), 1)
    return (col == row * N_TP + g).astype(f32)


def prepare_kernel(high_ref, low_ref, time_ref, shares_ref, *refs):
    *w_refs, hid_high_ref, hid_low_ref, gram_ref = refs
    pooled = shares_ref[0]
    for g in range(1, N_TP):
        pooled = pooled + shares_ref[g]
    pooled = pooled / PROMPT
    pooled = jnp.concatenate([pooled[k : k + 1] for k in range(D // 128)], axis=1)
    is_one = lax.broadcasted_iota(jnp.int32, (16, D), 0) == 0
    for net, w_ref in enumerate(w_refs):
        bias = jnp.broadcast_to(time_ref[net : net + 1, :] + pooled, (16, D))
        bias = jnp.where(is_one, bias, 0.0)
        for ref, table_ref, part in zip((hid_high_ref, hid_low_ref), (high_ref, low_ref), split2(bias)):
            ref[net, :CH, :] = w_ref[...] if ref is hid_high_ref else jnp.zeros((CH, D), bf16)
            ref[net, ROW0:ONE, :] = table_ref[:GRID_H]
            ref[net, ONE:COL0, :] = part
            ref[net, COL0:, :] = table_ref[GRID_H:]
        high, low = hid_high_ref[net], hid_low_ref[net]
        cross = nt(high, low)
        gram_ref[net] = nt(high, high) + cross + nt(low, high)


def project_kernel(pick_ref, hid_ref, w_ref, out_ref):
    out_ref[0] = nn(hid_ref[0], w_ref[0]).astype(bf16)


def project(pick, hid, w):
    return pl.pallas_call(
        project_kernel,
        grid_spec=pltpu.PrefetchScalarGridSpec(
            num_scalar_prefetch=1,
            grid=(3,),
            in_specs=[
                pl.BlockSpec((1, BASIS, D), lambda k, pick: (pick[1], 0, 0)),
                pl.BlockSpec((1, D, 128), lambda k, pick: (pick[0] + k, 0, 0)),
            ],
            out_specs=pl.BlockSpec((1, BASIS, 128), lambda k, pick: (k, 0, 0)),
        ),
        out_shape=jax.ShapeDtypeStruct((3, BASIS, 128), bf16),
        compiler_params=pltpu.CompilerParams(vmem_limit_bytes=VMEM),
        cost_estimate=pl.CostEstimate(flops=2 * BASIS * D * 384, bytes_accessed=3 * 10**6, transcendentals=0),
        name="project",
    )(pick, hid, w)


def attend_kernel(nets, members, packed, wout_at, place_ref, base_ref, *refs):
    if packed:
        z_ref, *refs = refs
    gram_ref, *refs = refs
    proj_refs = refs[:-9]
    wout_hbm, out_ref, x_ref, qp_ref, s_ref, sc_ref, wout_ref, z32_ref, sem = refs[-9:]
    s, xl, zh, core = place_ref[0], place_ref[2], place_ref[3], place_ref[4]
    shares = N_TP // members
    count = shares * OWN
    load = pltpu.make_async_copy(wout_hbm.at[pl.ds(wout_at, members * nets)], wout_ref, sem)
    load.start()
    if packed:
        z32_ref[...] = z_ref[...].astype(f32)
        for sec in range(N_SEC):
            unused, rest, hot = features(base_ref[sec])
            for j in range(OWN):
                at = (j * N_SEC + sec) * 16
                x_ref[at : at + 16, :128] = rest[j * 16 : (j + 1) * 16]
                x_ref[at : at + 16, COL0:] = hot[j * 16 : (j + 1) * 16]
        lane = lax.broadcasted_iota(jnp.int32, (256, 128), 1)
        for j in range(OWN):
            chunk = z32_ref[pl.ds(j // 2, 256, stride=8), :].astype(bf16)
            if j % 2:
                chunk = jnp.concatenate([chunk[:, 64:], chunk[:, :64]], axis=1)
            at = slice(j * 256, (j + 1) * 256)
            x_ref[at, :128] = jnp.where(lane < CH, chunk, x_ref[at, :128])
        own = jnp.concatenate(
            [x_ref[pl.ds(pl.multiple_of((j * N_SEC + s) * 16, 16), 16), :] for j in range(OWN)], axis=0
        )
        scales = z32_ref[pl.ds(6, 256, stride=8), :].T
        for net in range(nets):
            for j in range(OWN):
                line = net * 32 + j
                line = scales[line : line + 1] + scales[line + 16 : line + 17]
                at = j * 256
                sc_ref[net, at // KEYS, :, at % KEYS : at % KEYS + 256] = jnp.broadcast_to(line, (8, 256))
    else:
        for sec in range(N_SEC):
            z, rest, hot = features(base_ref[sec])
            lane = lax.broadcasted_iota(jnp.int32, z.shape, 1)
            x_ref[sec * LOCAL : (sec + 1) * LOCAL, :128] = jnp.where(lane < CH, z, rest)
            x_ref[sec * LOCAL : (sec + 1) * LOCAL, COL0:] = hot
        own = x_ref[pl.ds(pl.multiple_of(s * LOCAL, LOCAL), LOCAL), :]
    row = lax.broadcasted_iota(jnp.int32, (count, LOCAL), 0)
    col = lax.broadcasted_iota(jnp.int32, (count, LOCAL), 1)
    share = lax.shift_right_logical(row * 171, 11)
    if members == 2:
        owner = xl * 8 + share
    else:
        owner = lax.shift_right_logical(share, 1) * 8 + zh * 2 + lax.bitwise_and(share, 1)
    order = (col == (row - share * OWN) * N_TP + owner).astype(bf16)
    queries = nn(order, own).astype(bf16)
    eye = (
        lax.broadcasted_iota(jnp.int32, (BASIS, BASIS), 0) == lax.broadcasted_iota(jnp.int32, (BASIS, BASIS), 1)
    ).astype(bf16)
    heads = [(member, slice(half * HD, (half + 1) * HD)) for member in range(members) for half in range(2)]
    rows = len(heads) * count
    for turn in range(nets):
        net = lax.bitwise_xor(core, turn) if nets == 2 else 0
        gram_high, gram_low = split2(gram_ref[net])
        energy = jnp.sum(
            (nn(queries, gram_high) + nn(queries, gram_low)) * queries.astype(f32), axis=1, keepdims=True
        )
        scale = lax.rsqrt(energy / D + EPS)

        def proj(member, kind):
            if nets == 2:
                return proj_refs[turn][member, kind]
            return proj_refs[member][kind]

        for h, (member, part) in enumerate(heads):
            if part.start == 0:
                q = (nn(queries, proj(member, 0)) * scale).astype(bf16)
            qp_ref[h * count : (h + 1) * count, :] = (
                nt(q[:, part], proj(member, 1)[:, part]) * HD ** (-0.5)
            ).astype(bf16)

        def score(block, top):
            keys = x_ref[pl.ds(pl.multiple_of(block * KEYS, KEYS), KEYS), :]
            if not packed:
                energy = (nt(gram_high, keys) + nt(gram_low, keys)) * nt(eye, keys)
                scale = lax.rsqrt(jnp.sum(energy, axis=0, keepdims=True) / D + EPS)
                sc_ref[net, block] = jnp.broadcast_to(scale, (8, KEYS))
            scores = nt(qp_ref[...], keys) * sc_ref[net, block][:1]
            s_ref[block] = scores
            for part in range(KEYS // 128):
                top = jnp.maximum(top, scores[:, part * 128 : (part + 1) * 128])
            return top

        top = lax.fori_loop(0, TOKENS // KEYS, score, jnp.full((rows, 128), -1e30, f32))
        top = jnp.max(top, axis=1, keepdims=True)

        def mix(block, carry):
            total, mixed = carry
            expo = jnp.exp(s_ref[block] - top)
            for part in range(KEYS // 128):
                total = total + expo[:, part * 128 : (part + 1) * 128]
            weights = (expo * sc_ref[net, block][:1]).astype(bf16)
            keys = x_ref[pl.ds(pl.multiple_of(block * KEYS, KEYS), KEYS), :]
            return total, mixed + nn(weights, keys)

        total, mixed = lax.fori_loop(
            0, TOKENS // KEYS, mix, (jnp.zeros((rows, 128), f32), jnp.zeros((rows, BASIS), f32))
        )
        mixed = (mixed / jnp.sum(total, axis=1, keepdims=True)).astype(bf16)
        if turn == 0:
            load.wait()
        values = [
            nn(mixed[h * count : (h + 1) * count], proj(member, 2)[:, part]) for h, (member, part) in enumerate(heads)
        ]
        values = jnp.concatenate(values, axis=1).astype(bf16)
        term = []
        for part in range(4):
            at = slice(part * QUART, (part + 1) * QUART)
            term.append(nt(values, jnp.concatenate([wout_ref[m * nets + net, at, :] for m in range(members)], axis=1)))
        for d in range(shares):
            block = jnp.concatenate([t[d * OWN : (d + 1) * OWN] for t in term], axis=0).astype(bf16)
            if nets == 2:
                out_ref[d, pl.ds(pl.multiple_of(net * 48, 16), 48), :] = block
            else:
                out_ref[d] = block


def attend(place, base, z, gram_at, gram, proj, wout_at, wout):
    nets = 1 if z is None else 2
    members = 2 if z is None else 4
    packed = z is not None
    args = (base, z) if packed else (base,)
    rows = 2 * members * OWN * (N_TP // members)
    whole = lambda a: pl.BlockSpec(a.shape, lambda i: (0,) * a.ndim)
    out = jax.ShapeDtypeStruct((N_TP // members, nets * 4 * OWN, QUART), bf16)
    return pl.pallas_call(
        lambda *refs: attend_kernel(nets, members, packed, wout_at, *refs),
        out_shape=out,
        grid=(1,),
        in_specs=[pl.BlockSpec(memory_space=pltpu.SMEM)]
        + [whole(a) for a in args]
        + [pl.BlockSpec((nets, BASIS, BASIS), lambda i: (gram_at, 0, 0))]
        + [whole(a) for a in proj]
        + [pl.BlockSpec(memory_space=pl.ANY)],
        out_specs=whole(out),
        scratch_shapes=[
            pltpu.VMEM((TOKENS, BASIS), bf16),
            pltpu.VMEM((rows, BASIS), bf16),
            pltpu.VMEM((TOKENS // KEYS, rows, KEYS), f32),
            pltpu.VMEM((nets, TOKENS // KEYS, 8, KEYS), f32),
            pltpu.VMEM((members * nets, D, 128), bf16),
            pltpu.VMEM((N_SEC * N_TP * 8, 128), f32),
            pltpu.SemaphoreType.DMA,
        ],
        compiler_params=pltpu.CompilerParams(vmem_limit_bytes=VMEM),
        cost_estimate=pl.CostEstimate(flops=nets * 4 * 10**9, bytes_accessed=10**7, transcendentals=nets * 1200000),
        name="attend",
    )(place, *args, gram, *proj, wout)


def finish(recv_ref, net, hidden, w_final):
    rows = slice(net * 4 * OWN, (net + 1) * 4 * OWN)
    terms = recv_ref[0, rows].astype(f32)
    for d in range(1, recv_ref.shape[0]):
        terms = terms + recv_ref[d, rows].astype(f32)
    afters = []
    energy = jnp.zeros((OWN, 1), f32)
    for part in range(4):
        after = hidden[:, part * QUART : (part + 1) * QUART] + terms[part * OWN : (part + 1) * OWN]
        energy = energy + jnp.sum(after * after, axis=1, keepdims=True)
        afters.append(after)
    scale = lax.rsqrt(energy / D + EPS)
    normed = jnp.concatenate([after * scale for after in afters], axis=1).astype(bf16)
    return nt(normed, w_final[...])


def own_kernel(place_ref, message_ref, high_ref, low_ref, x12_ref, hidden_ref):
    z, rest, hot = features(message_ref[...])
    lane = lax.broadcasted_iota(jnp.int32, z.shape, 1)
    full = jnp.concatenate([jnp.where(lane < CH, z, rest), hot], axis=1)
    x12 = nn(own_tokens(place_ref[1]).astype(bf16), full).astype(bf16)
    x12_ref[...] = x12
    hidden_ref[...] = nn(x12, high_ref[0]) + nn(x12, low_ref[0])


def scores_own_kernel(after_ref, x12_ref, high_ref, low_ref, hidden_ref):
    for net in range(2):
        hidden_ref[net] = nn(x12_ref[...], high_ref[net]) + nn(x12_ref[...], low_ref[net])


def student_kernel(
    place_ref, time_ref, recv_ref, hidden_ref, own12_ref, noise_ref, renoise_ref, wf_ref, gram_ref,
    x0_ref, noisy_ref, x12_ref, send_ref,
):
    pick = own_tokens(place_ref[1])
    x12 = own12_ref[...]
    velocity = finish(recv_ref, 0, hidden_ref[...], wf_ref)
    exact = lax.Precision.HIGHEST
    noise = jnp.dot(pick, noise_ref[...], precision=exact, preferred_element_type=f32)
    renoise = jnp.dot(pick, renoise_ref[...], precision=exact, preferred_element_type=f32)
    x0 = noise - velocity
    t = time_ref[0]
    noisy = (1.0 - t) * x0 + t * renoise
    x12 = jnp.concatenate([noisy.astype(bf16), x12[:, CH:]], axis=1)
    x0_ref[...] = x0
    noisy_ref[...] = noisy
    x12_ref[...] = x12
    row = lax.broadcasted_iota(jnp.int32, (OWN, 128), 0)
    lane = lax.broadcasted_iota(jnp.int32, (OWN, 128), 1)
    scales = jnp.zeros((OWN, 128), f32)
    for net in range(2):
        high, low = split2(gram_ref[net])
        energy = jnp.sum((nn(x12, high) + nn(x12, low)) * x12.astype(f32), axis=1, keepdims=True)
        for part, value in enumerate(split2(lax.rsqrt(energy / D + EPS))):
            scales = jnp.where(lane == row + (net * 32 + part * 16), value.astype(f32), scales)
    scales = jnp.sum(scales, axis=0, keepdims=True)
    pairs = [jnp.concatenate([noisy[j : j + 1], noisy[j + 1 : j + 2]], axis=1) for j in range(0, OWN, 2)]
    send_ref[...] = jnp.concatenate(pairs + [scales, jnp.zeros((1, 128), f32)], axis=0).astype(bf16)


def score_kernel(
    time_ref, recv_ref, x0_ref, noisy_ref, hidden_ref, wr_ref, wf_ref, send_ref
):
    noisy = noisy_ref[...]
    real = finish(recv_ref, 0, hidden_ref[0], wr_ref)
    fake = finish(recv_ref, 1, hidden_ref[1], wf_ref)
    t = time_ref[0]
    gap = jnp.abs(x0_ref[...] - (noisy - t * real))
    gap = jnp.sum(jnp.sum(gap, axis=1, keepdims=True), axis=0, keepdims=True)
    grad = t * (real - fake)
    packed = [jnp.concatenate([grad[j : j + 1], grad[j + 1 : j + 2]], axis=1) for j in range(0, OWN, 2)]
    packed = jnp.concatenate([*packed, jnp.broadcast_to(gap, (1, 128)), jnp.zeros((1, 128), f32)], axis=0)
    send_ref[...] = jnp.broadcast_to(packed[None], send_ref.shape)


def call(kernel, shapes, smem, *args):
    def spec(arg):
        if isinstance(arg, tuple):
            array, n, at = arg
            return pl.BlockSpec((n, *array.shape[1:]), lambda i: (at,) + (0,) * (array.ndim - 1))
        return pl.BlockSpec(arg.shape, lambda i: (0,) * len(arg.shape))

    return pl.pallas_call(
        kernel,
        out_shape=shapes,
        grid=(1,),
        in_specs=[pl.BlockSpec(memory_space=pltpu.SMEM)] * smem + [spec(arg) for arg in args[smem:]],
        out_specs=jax.tree.map(spec, shapes),
        compiler_params=pltpu.CompilerParams(vmem_limit_bytes=VMEM),
        cost_estimate=pl.CostEstimate(flops=10**9, bytes_accessed=10**7, transcendentals=0),
        name=kernel.__name__,
    )(*[arg[0] if isinstance(arg, tuple) else arg for arg in args])


def swap(values, axes):
    return lax.all_to_all(values, axes, 0, 0, tiled=False)


def spread_to(values, axes, count):
    return swap(jnp.broadcast_to(values[None], (count, *values.shape)), axes)


def shift(values, axis, count, step):
    return lax.ppermute(values, axis, [((i + step) % count, i) for i in range(count)])


def place_tables():
    quarter = D // 4
    frequency = np.exp(-math.log(10000.0) * np.arange(quarter, dtype=np.float64) / quarter)
    table = np.zeros((GRID_H + GRID_W, D), np.float32)
    row = np.arange(GRID_H)[:, None] * frequency[None, :]
    col = np.arange(GRID_W)[:, None] * frequency[None, :]
    table[:GRID_H, : D // 2] = np.concatenate([np.sin(row), np.cos(row)], axis=1)
    table[GRID_H:, D // 2 :] = np.concatenate([np.sin(col), np.cos(col)], axis=1)
    high = table.astype(bf16)
    return jnp.asarray(high), jnp.asarray((table - high.astype(np.float32)).astype(bf16))


def time_embed(step_time):
    half_width = D // 2
    frequency = jnp.exp(-math.log(10000.0) * jnp.arange(half_width, dtype=f32) / half_width)
    angles = 1000.0 * step_time * frequency
    return jnp.concatenate([jnp.cos(angles), jnp.sin(angles)])


def per_device(
    student_noise,
    renoise_noise,
    patch_slot,
    renoise_step,
    prompt_ids,
    text_table,
    student_in,
    student_qkv,
    student_out,
    student_final,
    real_in,
    real_qkv,
    real_out,
    real_final,
    fake_in,
    fake_qkv,
    fake_out,
    fake_final,
):
    s = lax.axis_index(SEC)
    g = lax.axis_index(TP)
    core = lax.axis_index("core")
    place = jnp.stack([s, g, lax.axis_index("xl"), lax.axis_index("zh"), core]).astype(jnp.int32)
    step_time = renoise_step[0].astype(f32) / 1000.0

    vocab_local = text_table.shape[0]
    first_row = (s * N_TP + g) * vocab_local
    prompt_row = prompt_ids[0] - first_row
    matches = (prompt_row[:, None] == jnp.arange(vocab_local, dtype=jnp.int32)[None, :]).astype(f32)
    counts = jnp.sum(matches, axis=0).astype(bf16)
    partial_pool = nn(counts[None], text_table).reshape(D // 128, 128)
    noise = student_noise[0]
    packed = noise.astype(bf16)
    packed = jnp.concatenate([packed[:SLOTS], packed[SLOTS:]], axis=1)
    slot = patch_slot[0]
    lines = jnp.stack([slot // GRID_W, slot % GRID_W]).astype(bf16)
    lines = jnp.pad(jnp.pad(lines, ((0, 0), (0, 64))).reshape(4, 128), ((0, 4), (0, 0)))
    own = jnp.concatenate([packed, lines, *split2(partial_pool), jnp.zeros((2, 128), bf16)], axis=0)
    out_peer = shift(student_out, "xl", 2, 1)[None]
    out_peer, own = lax.optimization_barrier((out_peer, own))
    base = spread_to(own, SEC, N_SEC)
    out2 = jnp.stack([real_out, fake_out])
    out2, own = lax.optimization_barrier((out2, own))
    out2 = lax.all_gather(out2, "zh", axis=0, tiled=True)
    shares = base[:, SHARES : SHARES + 38].astype(f32).reshape(N_SEC * 2, D // 128, 128)
    shares = jnp.sum(shares, axis=0)
    shares, out2 = lax.optimization_barrier((shares, out2))
    shares = spread_to(shares, TP, N_TP)

    def columns(qkv):
        return jnp.transpose(qkv, (1, 0, 2))

    def gather(*parts):
        return lax.all_gather(jnp.concatenate(parts, axis=0), SEC, axis=1, tiled=True)

    first = gather(columns(student_qkv), student_out[None], out_peer)

    one = jax.ShapeDtypeStruct
    tables = place_tables()

    def prepare(shares, times, *w_in):
        n = len(w_in)
        shapes = (one((n, BASIS, D), bf16), one((n, BASIS, D), bf16), one((n, BASIS, BASIS), f32))
        return call(prepare_kernel, shapes, 0, *tables, jnp.stack([time_embed(t) for t in times]), shares, *w_in)

    high1, low1, gram1 = prepare(shares, (jnp.float32(1.0),), student_in)
    first, gram1 = lax.optimization_barrier((first, gram1))
    real_qkv, fake_qkv, out2, first = lax.optimization_barrier((real_qkv, fake_qkv, out2, first))
    second = gather(columns(real_qkv), columns(fake_qkv), out2)
    zero = jnp.int32(0)
    proj1 = project(jnp.stack([zero, zero]), high1, first)
    peer1 = shift(proj1, "xl", 2, 1)
    place, proj1 = lax.optimization_barrier((place, proj1))
    x12, hidden = call(
        own_kernel, (one((OWN, BASIS), bf16), one((OWN, D), f32)), 1, place, own, (high1, 1, 0), (low1, 1, 0)
    )
    place, hidden = lax.optimization_barrier((place, hidden))
    terms = attend(place, base, None, 0, gram1, (proj1, peer1), 3, first)
    shares, terms = lax.optimization_barrier((shares, terms))
    high, low, gram = prepare(shares, (step_time, step_time), real_in, fake_in)
    terms = swap(terms, ("zh", "zp"))
    terms, gram = lax.optimization_barrier((terms, gram))
    x0, noisy, x12, message = call(
        student_kernel,
        (one((OWN, CH), f32), one((OWN, CH), f32), one((OWN, BASIS), bf16), one((8, 128), bf16)),
        2,
        place,
        step_time[None],
        terms,
        hidden,
        x12,
        noise,
        renoise_noise[0],
        student_final.T,
        (gram, 2, 0),
    )
    pick = jnp.stack([3 * core, core])
    pick, message, second = lax.optimization_barrier((pick, message, second))
    proj2 = project(pick, high, second)
    near = spread_to(message, TP, N_TP).reshape(N_TP * 8, 128)
    near, proj2 = lax.optimization_barrier((near, proj2))
    proj2 = lax.all_gather(proj2, "zh", axis=0, tiled=False)
    everyone = spread_to(near, SEC, N_SEC).reshape(N_SEC * N_TP * 8, 128)
    proj2 = (proj2, shift(proj2, "core", 2, 1))
    terms = attend(place, base, everyone, 0, gram, proj2, 6, second)
    x12, terms = lax.optimization_barrier((x12, terms))
    hidden = call(
        scores_own_kernel, one((2, OWN, D), f32), 1, place, x12, (high, 2, 0), (low, 2, 0)
    )
    terms = swap(terms, ("xl", "zp"))
    message = call(
        score_kernel,
        one((N_TP, 8, 128), f32),
        1,
        step_time[None],
        terms,
        x0,
        noisy,
        hidden,
        real_final.T,
        fake_final.T,
    )
    near = swap(message, TP)
    gap = spread_to(jnp.sum(near[:, 6:7], axis=0), SEC, N_SEC)
    spread = jnp.sum(gap[:, 0, 0]) / (TOKENS * CH) + 1e-05
    grad = jnp.transpose(near[:, :6].reshape(N_TP, 6, 2, CH), (1, 2, 0, 3))
    return (grad.reshape(LOCAL, CH) / spread)[None]


def solution(mesh):
    fine = Mesh(mesh.devices.reshape(8, 2, 2, 4, 2, 2), ("y", "core", "xl", "zh", "zp", "rep"))
    qkv = P(SEC, None, TP)
    out = P(SEC, TP)
    net = (P(), qkv, out, P())
    placed = (
        P("rep", SEC, None),
        P("rep", SEC, None),
        P("rep", SEC),
        P("rep"),
        P("rep", None),
        P(SEC + TP, None),
    ) + net * 3
    return jax.shard_map(
        per_device, mesh=fine, in_specs=placed, out_specs=P("rep", SEC, None), check_vma=False
    )
```

```python
import math

import jax
import jax.numpy as jnp
import numpy as np
from jax import lax
from jax.experimental import pallas as pl
from jax.experimental.pallas import tpu as pltpu
from jax.sharding import Mesh, PartitionSpec as P

D = 2432
HD = 64
GRID_W = 64
GRID_H = 48
CH = 64
BASIS = 192
ROW0, ONE, COL0 = 64, 112, 128
EPS = 1e-06
SEC = ("y", "core")
TP = ("xl", "zh", "zp")
N_SEC = 16
PROMPT = 256
N_TP = 16
LOCAL = 192
OWN = 12
DESTS = 8
TOKENS = 3072
KEYS = 1536
QUART = D // 4
SLOTS, SHARES, MESSAGE = 96, 104, 144
VMEM = 60 * 2**20
bf16 = jnp.bfloat16
f32 = jnp.float32


def nn(a, b):
    return jnp.dot(a, b, preferred_element_type=f32)


def nt(a, b):
    return lax.dot_general(a, b, (((1,), (1,)), ((), ())), preferred_element_type=f32)


def split2(values):
    high = values.astype(bf16)
    return high, (values - high.astype(f32)).astype(bf16)


def features(message):
    z = message[:SLOTS]
    z = jnp.concatenate([z, jnp.concatenate([z[:, CH:], z[:, :CH]], axis=1)], axis=0)
    slots = message[SLOTS:SHARES].astype(f32).T
    row = jnp.concatenate([slots[:, 0:1], slots[:64, 1:2]], axis=0)
    col = jnp.concatenate([slots[:, 2:3], slots[:64, 3:4]], axis=0)
    lane = lax.broadcasted_iota(jnp.int32, (LOCAL, 128), 1).astype(f32)
    rest = ((lane == row + ROW0) | (lane == ONE)).astype(f32).astype(bf16)
    hot = (lane[:, :GRID_W] == col).astype(f32).astype(bf16)
    return z, rest, hot


def own_tokens(g):
    row = lax.broadcasted_iota(jnp.int32, (OWN, LOCAL), 0)
    col = lax.broadcasted_iota(jnp.int32, (OWN, LOCAL), 1)
    return (col == row * N_TP + g).astype(f32)


def prepare_kernel(high_ref, low_ref, time_ref, shares_ref, *refs):
    *w_refs, hid_high_ref, hid_low_ref, gram_ref = refs
    pooled = shares_ref[0]
    for g in range(1, N_TP):
        pooled = pooled + shares_ref[g]
    pooled = pooled / PROMPT
    pooled = jnp.concatenate([pooled[k : k + 1] for k in range(D // 128)], axis=1)
    is_one = lax.broadcasted_iota(jnp.int32, (16, D), 0) == 0
    for net, w_ref in enumerate(w_refs):
        bias = jnp.broadcast_to(time_ref[net : net + 1, :] + pooled, (16, D))
        bias = jnp.where(is_one, bias, 0.0)
        for ref, table_ref, part in zip((hid_high_ref, hid_low_ref), (high_ref, low_ref), split2(bias)):
            ref[net, :CH, :] = w_ref[...] if ref is hid_high_ref else jnp.zeros((CH, D), bf16)
            ref[net, ROW0:ONE, :] = table_ref[:GRID_H]
            ref[net, ONE:COL0, :] = part
            ref[net, COL0:, :] = table_ref[GRID_H:]
        high, low = hid_high_ref[net], hid_low_ref[net]
        cross = nt(high, low)
        gram_ref[net] = nt(high, high) + cross + nt(low, high)


def project_kernel(pick_ref, hid_ref, w_ref, out_ref):
    out = nn(hid_ref[0], jnp.concatenate([w_ref[k] for k in range(3)], axis=1)).astype(bf16)
    for k in range(3):
        out_ref[k] = out[:, k * 128 : (k + 1) * 128]


def project(pick, hid, w):
    return pl.pallas_call(
        project_kernel,
        grid_spec=pltpu.PrefetchScalarGridSpec(
            num_scalar_prefetch=1,
            grid=(1,),
            in_specs=[
                pl.BlockSpec((1, BASIS, D), lambda i, pick: (pick[0], 0, 0)),
                pl.BlockSpec((3, D, 128), lambda i, pick: (pick[0], 0, 0)),
            ],
            out_specs=pl.BlockSpec((3, BASIS, 128), lambda i, pick: (0, 0, 0)),
        ),
        out_shape=jax.ShapeDtypeStruct((3, BASIS, 128), bf16),
        compiler_params=pltpu.CompilerParams(vmem_limit_bytes=VMEM),
        cost_estimate=pl.CostEstimate(flops=2 * BASIS * D * 384, bytes_accessed=3 * 10**6, transcendentals=0),
        name="project",
    )(pick, hid, w)


def attend_kernel(members, packed, wout_at, place_ref, base_ref, *refs):
    if packed:
        z_ref, *refs = refs
    gram_ref, *refs = refs
    proj_refs = refs[:-9]
    wout_hbm, out_ref, x_ref, qp_ref, s_ref, sc_ref, wout_ref, z32_ref, sem = refs[-9:]
    s, xl, zh, core = place_ref[0], place_ref[2], place_ref[3], place_ref[4]
    count = DESTS * OWN
    net = core if packed else 0
    loads = [
        pltpu.make_async_copy(wout_hbm.at[wout_at + (2 * m + net if packed else m)], wout_ref.at[m], sem.at[m])
        for m in range(members)
    ]
    for load in loads:
        load.start()
    if packed:
        z32_ref[...] = z_ref[...].astype(f32)
        for sec in range(N_SEC):
            unused, rest, hot = features(base_ref[sec])
            for j in range(OWN):
                at = (j * N_SEC + sec) * 16
                x_ref[at : at + 16, :128] = rest[j * 16 : (j + 1) * 16]
                x_ref[at : at + 16, COL0:] = hot[j * 16 : (j + 1) * 16]
        lane = lax.broadcasted_iota(jnp.int32, (256, 128), 1)
        for j in range(OWN):
            chunk = z32_ref[pl.ds(j // 2, 256, stride=8), :].astype(bf16)
            if j % 2:
                chunk = jnp.concatenate([chunk[:, 64:], chunk[:, :64]], axis=1)
            at = slice(j * 256, (j + 1) * 256)
            x_ref[at, :128] = jnp.where(lane < CH, chunk, x_ref[at, :128])
        own = jnp.concatenate(
            [
                x_ref[pl.ds(pl.multiple_of((j * N_SEC + s - core + other) * 16, 16), 16), :]
                for other in range(2)
                for j in range(OWN)
            ],
            axis=0,
        )
        scales = z32_ref[pl.ds(6, 256, stride=8), :].T
        scales = jnp.where(core == 0, scales[:32], scales[32:64])
        for j in range(OWN):
            line = scales[j : j + 1] + scales[j + 16 : j + 17]
            at = j * 256
            sc_ref[at // KEYS, :, at % KEYS : at % KEYS + 256] = jnp.broadcast_to(line, (8, 256))
    else:
        for sec in range(N_SEC):
            z, rest, hot = features(base_ref[sec])
            lane = lax.broadcasted_iota(jnp.int32, z.shape, 1)
            x_ref[sec * LOCAL : (sec + 1) * LOCAL, :128] = jnp.where(lane < CH, z, rest)
            x_ref[sec * LOCAL : (sec + 1) * LOCAL, COL0:] = hot
        own = x_ref[pl.ds(pl.multiple_of(s * LOCAL, LOCAL), LOCAL), :]
    row = lax.broadcasted_iota(jnp.int32, (count, own.shape[0]), 0)
    col = lax.broadcasted_iota(jnp.int32, (count, own.shape[0]), 1)
    share = lax.shift_right_logical(row * 171, 11)
    token = row - share * OWN
    if packed:
        half = lax.shift_right_logical(share, 2)
        owner = lax.bitwise_and(lax.shift_right_logical(share, 1), 1) * 8 + zh * 2 + lax.bitwise_and(share, 1)
        order = (col == half * LOCAL + token * N_TP + owner).astype(bf16)
    else:
        order = (col == token * N_TP + xl * 8 + share).astype(bf16)
    queries = nn(order, own).astype(bf16)
    eye = (
        lax.broadcasted_iota(jnp.int32, (BASIS, BASIS), 0) == lax.broadcasted_iota(jnp.int32, (BASIS, BASIS), 1)
    ).astype(bf16)
    heads = [(member, slice(half * HD, (half + 1) * HD)) for member in range(members) for half in range(2)]
    rows = len(heads) * count
    gram_high, gram_low = split2(gram_ref[net])
    energy = jnp.sum(
        (nn(queries, gram_high) + nn(queries, gram_low)) * queries.astype(f32), axis=1, keepdims=True
    )
    scale = lax.rsqrt(energy / D + EPS)

    def proj(member, kind):
        return proj_refs[0][member, kind] if packed else proj_refs[member][kind]

    for h, (member, part) in enumerate(heads):
        if part.start == 0:
            q = (nn(queries, proj(member, 0)) * scale).astype(bf16)
        qp_ref[h * count : (h + 1) * count, :] = (
            nt(q[:, part], proj(member, 1)[:, part]) * HD ** (-0.5)
        ).astype(bf16)

    def score(block, top):
        keys = x_ref[pl.ds(pl.multiple_of(block * KEYS, KEYS), KEYS), :]
        if not packed:
            energy = (nt(gram_high, keys) + nt(gram_low, keys)) * nt(eye, keys)
            scale = lax.rsqrt(jnp.sum(energy, axis=0, keepdims=True) / D + EPS)
            sc_ref[block] = jnp.broadcast_to(scale, (8, KEYS))
        scores = nt(qp_ref[...], keys) * sc_ref[block][:1]
        s_ref[block] = scores
        for part in range(KEYS // 128):
            top = jnp.maximum(top, scores[:, part * 128 : (part + 1) * 128])
        return top

    top = lax.fori_loop(0, TOKENS // KEYS, score, jnp.full((rows, 128), -1e30, f32))
    top = jnp.max(top, axis=1, keepdims=True)

    def mix(block, carry):
        total, mixed = carry
        expo = jnp.exp(s_ref[block] - top)
        for part in range(KEYS // 128):
            total = total + expo[:, part * 128 : (part + 1) * 128]
        weights = (expo * sc_ref[block][:1]).astype(bf16)
        keys = x_ref[pl.ds(pl.multiple_of(block * KEYS, KEYS), KEYS), :]
        return total, mixed + nn(weights, keys)

    total, mixed = lax.fori_loop(
        0, TOKENS // KEYS, mix, (jnp.zeros((rows, 128), f32), jnp.zeros((rows, BASIS), f32))
    )
    mixed = (mixed / jnp.sum(total, axis=1, keepdims=True)).astype(bf16)
    for load in loads:
        load.wait()
    values = [
        nn(mixed[h * count : (h + 1) * count], proj(member, 2)[:, part]) for h, (member, part) in enumerate(heads)
    ]
    values = jnp.concatenate(values, axis=1).astype(bf16)
    term = []
    for part in range(4):
        at = slice(part * QUART, (part + 1) * QUART)
        term.append(nt(values, jnp.concatenate([wout_ref[m, at, :] for m in range(members)], axis=1)))
    for d in range(DESTS):
        out_ref[d] = jnp.concatenate([t[d * OWN : (d + 1) * OWN] for t in term], axis=0).astype(bf16)


def attend(place, base, z, gram, proj, wout_at, wout):
    packed = z is not None
    members = 4 if packed else 2
    args = (base, z) if packed else (base,)
    rows = 2 * members * DESTS * OWN
    whole = lambda a: pl.BlockSpec(a.shape, lambda i: (0,) * a.ndim)
    out = jax.ShapeDtypeStruct((DESTS, 4 * OWN, QUART), bf16)
    return pl.pallas_call(
        lambda *refs: attend_kernel(members, packed, wout_at, *refs),
        out_shape=out,
        grid=(1,),
        in_specs=[pl.BlockSpec(memory_space=pltpu.SMEM)]
        + [whole(a) for a in (*args, gram, *proj)]
        + [pl.BlockSpec(memory_space=pl.ANY)],
        out_specs=whole(out),
        scratch_shapes=[
            pltpu.VMEM((TOKENS, BASIS), bf16),
            pltpu.VMEM((rows, BASIS), bf16),
            pltpu.VMEM((TOKENS // KEYS, rows, KEYS), f32),
            pltpu.VMEM((TOKENS // KEYS, 8, KEYS), f32),
            pltpu.VMEM((members, D, 128), bf16),
            pltpu.VMEM((N_SEC * N_TP * 8, 128), f32),
            pltpu.SemaphoreType.DMA((members,)),
        ],
        compiler_params=pltpu.CompilerParams(vmem_limit_bytes=VMEM),
        cost_estimate=pl.CostEstimate(flops=members * 2 * 10**9, bytes_accessed=10**7, transcendentals=rows * TOKENS),
        name="attend",
    )(place, *args, gram, *proj, wout)


def finish(recv_ref, senders, hidden, w_final):
    terms = recv_ref[senders[0]].astype(f32)
    for d in senders[1:]:
        terms = terms + recv_ref[d].astype(f32)
    afters = []
    energy = jnp.zeros((OWN, 1), f32)
    for part in range(4):
        after = hidden[:, part * QUART : (part + 1) * QUART] + terms[part * OWN : (part + 1) * OWN]
        energy = energy + jnp.sum(after * after, axis=1, keepdims=True)
        afters.append(after)
    scale = lax.rsqrt(energy / D + EPS)
    normed = jnp.concatenate([after * scale for after in afters], axis=1).astype(bf16)
    return nt(normed, w_final[...])


def own_kernel(place_ref, message_ref, high_ref, low_ref, x12_ref, hidden_ref):
    z, rest, hot = features(message_ref[...])
    lane = lax.broadcasted_iota(jnp.int32, z.shape, 1)
    full = jnp.concatenate([jnp.where(lane < CH, z, rest), hot], axis=1)
    x12 = nn(own_tokens(place_ref[1]).astype(bf16), full).astype(bf16)
    x12_ref[...] = x12
    hidden_ref[...] = nn(x12, high_ref[0]) + nn(x12, low_ref[0])


def scores_own_kernel(after_ref, x12_ref, high_ref, low_ref, hidden_ref):
    for net in range(2):
        hidden_ref[net] = nn(x12_ref[...], high_ref[net]) + nn(x12_ref[...], low_ref[net])


def student_kernel(
    place_ref, time_ref, recv_ref, hidden_ref, own12_ref, noise_ref, renoise_ref, wf_ref, gram_ref,
    x0_ref, noisy_ref, x12_ref, send_ref,
):
    pick = own_tokens(place_ref[1])
    x12 = own12_ref[...]
    velocity = finish(recv_ref, range(DESTS), hidden_ref[...], wf_ref)
    exact = lax.Precision.HIGHEST
    noise = jnp.dot(pick, noise_ref[...], precision=exact, preferred_element_type=f32)
    renoise = jnp.dot(pick, renoise_ref[...], precision=exact, preferred_element_type=f32)
    x0 = noise - velocity
    t = time_ref[0]
    noisy = (1.0 - t) * x0 + t * renoise
    x12 = jnp.concatenate([noisy.astype(bf16), x12[:, CH:]], axis=1)
    x0_ref[...] = x0
    noisy_ref[...] = noisy
    x12_ref[...] = x12
    row = lax.broadcasted_iota(jnp.int32, (OWN, 128), 0)
    lane = lax.broadcasted_iota(jnp.int32, (OWN, 128), 1)
    scales = jnp.zeros((OWN, 128), f32)
    for net in range(2):
        high, low = split2(gram_ref[net])
        energy = jnp.sum((nn(x12, high) + nn(x12, low)) * x12.astype(f32), axis=1, keepdims=True)
        for part, value in enumerate(split2(lax.rsqrt(energy / D + EPS))):
            scales = jnp.where(lane == row + (net * 32 + part * 16), value.astype(f32), scales)
    scales = jnp.sum(scales, axis=0, keepdims=True)
    pairs = [jnp.concatenate([noisy[j : j + 1], noisy[j + 1 : j + 2]], axis=1) for j in range(0, OWN, 2)]
    send_ref[...] = jnp.concatenate(pairs + [scales, jnp.zeros((1, 128), f32)], axis=0).astype(bf16)


def score_kernel(
    time_ref, recv_ref, x0_ref, noisy_ref, hidden_ref, wr_ref, wf_ref, send_ref
):
    noisy = noisy_ref[...]
    real = finish(recv_ref, range(4), hidden_ref[0], wr_ref)
    fake = finish(recv_ref, range(4, DESTS), hidden_ref[1], wf_ref)
    t = time_ref[0]
    gap = jnp.abs(x0_ref[...] - (noisy - t * real))
    gap = jnp.sum(jnp.sum(gap, axis=1, keepdims=True), axis=0, keepdims=True)
    grad = t * (real - fake)
    packed = [jnp.concatenate([grad[j : j + 1], grad[j + 1 : j + 2]], axis=1) for j in range(0, OWN, 2)]
    packed = jnp.concatenate([*packed, jnp.broadcast_to(gap, (1, 128)), jnp.zeros((1, 128), f32)], axis=0)
    send_ref[...] = jnp.broadcast_to(packed[None], send_ref.shape)


def call(kernel, shapes, smem, *args):
    def spec(arg):
        if isinstance(arg, tuple):
            array, n, at = arg
            return pl.BlockSpec((n, *array.shape[1:]), lambda i: (at,) + (0,) * (array.ndim - 1))
        return pl.BlockSpec(arg.shape, lambda i: (0,) * len(arg.shape))

    return pl.pallas_call(
        kernel,
        out_shape=shapes,
        grid=(1,),
        in_specs=[pl.BlockSpec(memory_space=pltpu.SMEM)] * smem + [spec(arg) for arg in args[smem:]],
        out_specs=jax.tree.map(spec, shapes),
        compiler_params=pltpu.CompilerParams(vmem_limit_bytes=VMEM),
        cost_estimate=pl.CostEstimate(flops=10**9, bytes_accessed=10**7, transcendentals=0),
        name=kernel.__name__,
    )(*[arg[0] if isinstance(arg, tuple) else arg for arg in args])


def swap(values, axes):
    return lax.all_to_all(values, axes, 0, 0, tiled=False)


def spread_to(values, axes, count):
    return swap(jnp.broadcast_to(values[None], (count, *values.shape)), axes)


def shift(values, axis, count, step):
    return lax.ppermute(values, axis, [((i + step) % count, i) for i in range(count)])


def place_tables():
    quarter = D // 4
    frequency = np.exp(-math.log(10000.0) * np.arange(quarter, dtype=np.float64) / quarter)
    table = np.zeros((GRID_H + GRID_W, D), np.float32)
    row = np.arange(GRID_H)[:, None] * frequency[None, :]
    col = np.arange(GRID_W)[:, None] * frequency[None, :]
    table[:GRID_H, : D // 2] = np.concatenate([np.sin(row), np.cos(row)], axis=1)
    table[GRID_H:, D // 2 :] = np.concatenate([np.sin(col), np.cos(col)], axis=1)
    high = table.astype(bf16)
    return jnp.asarray(high), jnp.asarray((table - high.astype(np.float32)).astype(bf16))


def time_embed(step_time):
    half_width = D // 2
    frequency = jnp.exp(-math.log(10000.0) * jnp.arange(half_width, dtype=f32) / half_width)
    angles = 1000.0 * step_time * frequency
    return jnp.concatenate([jnp.cos(angles), jnp.sin(angles)])


def per_device(
    student_noise,
    renoise_noise,
    patch_slot,
    renoise_step,
    prompt_ids,
    text_table,
    student_in,
    student_qkv,
    student_out,
    student_final,
    real_in,
    real_qkv,
    real_out,
    real_final,
    fake_in,
    fake_qkv,
    fake_out,
    fake_final,
):
    s = lax.axis_index(SEC)
    g = lax.axis_index(TP)
    core = lax.axis_index("core").astype(jnp.int32)
    place = jnp.stack([s, g, lax.axis_index("xl"), lax.axis_index("zh"), core]).astype(jnp.int32)
    step_time = renoise_step[0].astype(f32) / 1000.0

    vocab_local = text_table.shape[0]
    first_row = (s * N_TP + g) * vocab_local
    prompt_row = prompt_ids[0] - first_row
    matches = (prompt_row[:, None] == jnp.arange(vocab_local, dtype=jnp.int32)[None, :]).astype(f32)
    counts = jnp.sum(matches, axis=0).astype(bf16)
    partial_pool = nn(counts[None], text_table).reshape(D // 128, 128)
    noise = student_noise[0]
    packed = noise.astype(bf16)
    packed = jnp.concatenate([packed[:SLOTS], packed[SLOTS:]], axis=1)
    slot = patch_slot[0]
    lines = jnp.stack([slot // GRID_W, slot % GRID_W]).astype(bf16)
    lines = jnp.pad(jnp.pad(lines, ((0, 0), (0, 64))).reshape(4, 128), ((0, 4), (0, 0)))
    own = jnp.concatenate([packed, lines, *split2(partial_pool), jnp.zeros((2, 128), bf16)], axis=0)
    out_peer = shift(student_out, "xl", 2, 1)[None]
    out_peer, own = lax.optimization_barrier((out_peer, own))
    base = spread_to(own, SEC, N_SEC)
    out2 = jnp.stack([real_out, fake_out])
    out2, own = lax.optimization_barrier((out2, own))
    out2 = lax.all_gather(out2, "zh", axis=0, tiled=True)
    shares = base[:, SHARES : SHARES + 38].astype(f32).reshape(N_SEC * 2, D // 128, 128)
    shares = jnp.sum(shares, axis=0)
    shares, out2 = lax.optimization_barrier((shares, out2))
    shares = spread_to(shares, TP, N_TP)

    def columns(qkv):
        return jnp.transpose(qkv, (1, 0, 2))

    def gather(*parts):
        return lax.all_gather(jnp.concatenate(parts, axis=0), SEC, axis=1, tiled=True)

    first = gather(columns(student_qkv), student_out[None], out_peer)

    one = jax.ShapeDtypeStruct
    tables = place_tables()

    def prepare(shares, times, *w_in):
        n = len(w_in)
        shapes = (one((n, BASIS, D), bf16), one((n, BASIS, D), bf16), one((n, BASIS, BASIS), f32))
        return call(prepare_kernel, shapes, 0, *tables, jnp.stack([time_embed(t) for t in times]), shares, *w_in)

    high1, low1, gram1 = prepare(shares, (jnp.float32(1.0),), student_in)
    first, gram1 = lax.optimization_barrier((first, gram1))
    real_qkv, fake_qkv, out2, first = lax.optimization_barrier((real_qkv, fake_qkv, out2, first))
    second = gather(columns(real_qkv), columns(fake_qkv), out2)
    proj1 = project(jnp.zeros((1,), jnp.int32), high1, first)
    peer1 = shift(proj1, "xl", 2, 1)
    place, proj1 = lax.optimization_barrier((place, proj1))
    x12, hidden = call(
        own_kernel, (one((OWN, BASIS), bf16), one((OWN, D), f32)), 1, place, own, (high1, 1, 0), (low1, 1, 0)
    )
    place, hidden = lax.optimization_barrier((place, hidden))
    terms = attend(place, base, None, gram1, (proj1, peer1), 3, first)
    shares, terms = lax.optimization_barrier((shares, terms))
    high, low, gram = prepare(shares, (step_time, step_time), real_in, fake_in)
    terms = swap(terms, ("zh", "zp"))
    terms, gram = lax.optimization_barrier((terms, gram))
    x0, noisy, x12, message = call(
        student_kernel,
        (one((OWN, CH), f32), one((OWN, CH), f32), one((OWN, BASIS), bf16), one((8, 128), bf16)),
        2,
        place,
        step_time[None],
        terms,
        hidden,
        x12,
        noise,
        renoise_noise[0],
        student_final.T,
        (gram, 2, 0),
    )
    pick, second, unused = lax.optimization_barrier((core[None], second, message))
    proj2 = project(pick, high, second)
    near = spread_to(message, TP, N_TP).reshape(N_TP * 8, 128)
    near, proj2 = lax.optimization_barrier((near, proj2))
    proj2 = lax.all_gather(proj2, "zh", axis=0, tiled=False)
    everyone = spread_to(near, SEC, N_SEC).reshape(N_SEC * N_TP * 8, 128)
    terms = attend(place, base, everyone, gram, (proj2,), 6, second)
    x12, terms = lax.optimization_barrier((x12, terms))
    hidden = call(
        scores_own_kernel, one((2, OWN, D), f32), 1, place, x12, (high, 2, 0), (low, 2, 0)
    )
    terms = swap(terms, ("core", "xl", "zp"))
    message = call(
        score_kernel,
        one((N_TP, 8, 128), f32),
        1,
        step_time[None],
        terms,
        x0,
        noisy,
        hidden,
        real_final.T,
        fake_final.T,
    )
    near = swap(message, TP)
    gap = spread_to(jnp.sum(near[:, 6:7], axis=0), SEC, N_SEC)
    spread = jnp.sum(gap[:, 0, 0]) / (TOKENS * CH) + 1e-05
    grad = jnp.transpose(near[:, :6].reshape(N_TP, 6, 2, CH), (1, 2, 0, 3))
    return (grad.reshape(LOCAL, CH) / spread)[None]


def solution(mesh):
    fine = Mesh(mesh.devices.reshape(8, 2, 2, 4, 2, 2), ("y", "core", "xl", "zh", "zp", "rep"))
    qkv = P(SEC, None, TP)
    out = P(SEC, TP)
    net = (P(), qkv, out, P())
    placed = (
        P("rep", SEC, None),
        P("rep", SEC, None),
        P("rep", SEC),
        P("rep"),
        P("rep", None),
        P(SEC + TP, None),
    ) + net * 3
    return jax.shard_map(
        per_device, mesh=fine, in_specs=placed, out_specs=P("rep", SEC, None), check_vma=False
    )
```

```python
import math

import jax
import jax.numpy as jnp
import numpy as np
from jax import lax
from jax.experimental import pallas as pl
from jax.experimental.pallas import tpu as pltpu
from jax.sharding import Mesh, PartitionSpec as P

D = 2432
HD = 64
GRID_W = 64
GRID_H = 48
CH = 64
BASIS = 192
ROW0, ONE, COL0 = 64, 112, 128
EPS = 1e-06
SEC = ("y", "core")
TP = ("xl", "zh", "zp")
N_SEC = 16
PROMPT = 256
N_TP = 16
LOCAL = 192
OWN = 12
DESTS = 8
TOKENS = 3072
KEYS = 1536
QUART = D // 4
SLOTS, SHARES, MESSAGE = 96, 104, 144
VMEM = 60 * 2**20
bf16 = jnp.bfloat16
f32 = jnp.float32


def nn(a, b):
    return jnp.dot(a, b, preferred_element_type=f32)


def nt(a, b):
    return lax.dot_general(a, b, (((1,), (1,)), ((), ())), preferred_element_type=f32)


def split2(values):
    high = values.astype(bf16)
    return high, (values - high.astype(f32)).astype(bf16)


def features(message):
    z = message[:SLOTS]
    z = jnp.concatenate([z, jnp.concatenate([z[:, CH:], z[:, :CH]], axis=1)], axis=0)
    slots = message[SLOTS:SHARES].astype(f32).T
    row = jnp.concatenate([slots[:, 0:1], slots[:64, 1:2]], axis=0)
    col = jnp.concatenate([slots[:, 2:3], slots[:64, 3:4]], axis=0)
    lane = lax.broadcasted_iota(jnp.int32, (LOCAL, 128), 1).astype(f32)
    rest = ((lane == row + ROW0) | (lane == ONE)).astype(f32).astype(bf16)
    hot = (lane[:, :GRID_W] == col).astype(f32).astype(bf16)
    return z, rest, hot


def own_tokens(g):
    row = lax.broadcasted_iota(jnp.int32, (OWN, LOCAL), 0)
    col = lax.broadcasted_iota(jnp.int32, (OWN, LOCAL), 1)
    return (col == row * N_TP + g).astype(f32)


def prepare_kernel(high_ref, low_ref, time_ref, shares_ref, *refs):
    *w_refs, hid_high_ref, hid_low_ref, gram_ref = refs
    pooled = shares_ref[0]
    for g in range(1, N_TP):
        pooled = pooled + shares_ref[g]
    pooled = pooled / PROMPT
    pooled = jnp.concatenate([pooled[k : k + 1] for k in range(D // 128)], axis=1)
    is_one = lax.broadcasted_iota(jnp.int32, (16, D), 0) == 0
    for net, w_ref in enumerate(w_refs):
        bias = jnp.broadcast_to(time_ref[net : net + 1, :] + pooled, (16, D))
        bias = jnp.where(is_one, bias, 0.0)
        for ref, table_ref, part in zip((hid_high_ref, hid_low_ref), (high_ref, low_ref), split2(bias)):
            ref[net, :CH, :] = w_ref[...] if ref is hid_high_ref else jnp.zeros((CH, D), bf16)
            ref[net, ROW0:ONE, :] = table_ref[:GRID_H]
            ref[net, ONE:COL0, :] = part
            ref[net, COL0:, :] = table_ref[GRID_H:]
        high, low = hid_high_ref[net], hid_low_ref[net]
        cross = nt(high, low)
        gram_ref[net] = nt(high, high) + cross + nt(low, high)


def project_kernel(pick_ref, hid_ref, w_ref, out_ref):
    out = nn(hid_ref[0], jnp.concatenate([w_ref[k] for k in range(3)], axis=1)).astype(bf16)
    for k in range(3):
        out_ref[k] = out[:, k * 128 : (k + 1) * 128]


def project(pick, hid, w):
    return pl.pallas_call(
        project_kernel,
        grid_spec=pltpu.PrefetchScalarGridSpec(
            num_scalar_prefetch=1,
            grid=(1,),
            in_specs=[
                pl.BlockSpec((1, BASIS, D), lambda i, pick: (pick[0], 0, 0)),
                pl.BlockSpec((3, D, 128), lambda i, pick: (pick[1], 0, 0)),
            ],
            out_specs=pl.BlockSpec((3, BASIS, 128), lambda i, pick: (0, 0, 0)),
        ),
        out_shape=jax.ShapeDtypeStruct((3, BASIS, 128), bf16),
        compiler_params=pltpu.CompilerParams(vmem_limit_bytes=VMEM),
        cost_estimate=pl.CostEstimate(flops=2 * BASIS * D * 384, bytes_accessed=3 * 10**6, transcendentals=0),
        name="project",
    )(pick, hid, w)


def attend_kernel(members, packed, wout_at, place_ref, base_ref, *refs):
    if packed:
        z_ref, *refs = refs
    gram_ref, *refs = refs
    proj_refs = refs[:-9]
    wout_hbm, out_ref, x_ref, qp_ref, s_ref, sc_ref, wout_ref, z32_ref, sem = refs[-9:]
    s, xl, zh, core = place_ref[0], place_ref[2], place_ref[3], place_ref[4]
    count = DESTS * OWN
    net = core if packed else 0
    loads = [
        pltpu.make_async_copy(wout_hbm.at[wout_at + m], wout_ref.at[m], sem.at[m])
        for m in range(members)
    ]
    for load in loads:
        load.start()
    if packed:
        z32_ref[...] = z_ref[...].astype(f32)
        for sec in range(N_SEC):
            unused, rest, hot = features(base_ref[sec])
            for j in range(OWN):
                at = (j * N_SEC + sec) * 16
                x_ref[at : at + 16, :128] = rest[j * 16 : (j + 1) * 16]
                x_ref[at : at + 16, COL0:] = hot[j * 16 : (j + 1) * 16]
        lane = lax.broadcasted_iota(jnp.int32, (256, 128), 1)
        for j in range(OWN):
            chunk = z32_ref[pl.ds(j // 2, 256, stride=8), :].astype(bf16)
            if j % 2:
                chunk = jnp.concatenate([chunk[:, 64:], chunk[:, :64]], axis=1)
            at = slice(j * 256, (j + 1) * 256)
            x_ref[at, :128] = jnp.where(lane < CH, chunk, x_ref[at, :128])
        own = jnp.concatenate(
            [
                x_ref[pl.ds(pl.multiple_of((j * N_SEC + s - core + other) * 16, 16), 16), :]
                for other in range(2)
                for j in range(OWN)
            ],
            axis=0,
        )
        scales = z32_ref[pl.ds(6, 256, stride=8), :].T
        scales = jnp.where(core == 0, scales[:32], scales[32:64])
        for j in range(OWN):
            line = scales[j : j + 1] + scales[j + 16 : j + 17]
            at = j * 256
            sc_ref[at // KEYS, :, at % KEYS : at % KEYS + 256] = jnp.broadcast_to(line, (8, 256))
    else:
        for sec in range(N_SEC):
            z, rest, hot = features(base_ref[sec])
            lane = lax.broadcasted_iota(jnp.int32, z.shape, 1)
            x_ref[sec * LOCAL : (sec + 1) * LOCAL, :128] = jnp.where(lane < CH, z, rest)
            x_ref[sec * LOCAL : (sec + 1) * LOCAL, COL0:] = hot
        own = x_ref[pl.ds(pl.multiple_of(s * LOCAL, LOCAL), LOCAL), :]
    row = lax.broadcasted_iota(jnp.int32, (count, own.shape[0]), 0)
    col = lax.broadcasted_iota(jnp.int32, (count, own.shape[0]), 1)
    share = lax.shift_right_logical(row * 171, 11)
    token = row - share * OWN
    if packed:
        half = lax.shift_right_logical(share, 2)
        owner = lax.bitwise_and(lax.shift_right_logical(share, 1), 1) * 8 + zh * 2 + lax.bitwise_and(share, 1)
        order = (col == half * LOCAL + token * N_TP + owner).astype(bf16)
    else:
        order = (col == token * N_TP + xl * 8 + share).astype(bf16)
    queries = nn(order, own).astype(bf16)
    eye = (
        lax.broadcasted_iota(jnp.int32, (BASIS, BASIS), 0) == lax.broadcasted_iota(jnp.int32, (BASIS, BASIS), 1)
    ).astype(bf16)
    heads = [(member, slice(half * HD, (half + 1) * HD)) for member in range(members) for half in range(2)]
    rows = len(heads) * count
    gram_high, gram_low = split2(gram_ref[net])
    energy = jnp.sum(
        (nn(queries, gram_high) + nn(queries, gram_low)) * queries.astype(f32), axis=1, keepdims=True
    )
    scale = lax.rsqrt(energy / D + EPS)

    def proj(member, kind):
        return proj_refs[0][member, kind] if packed else proj_refs[member][kind]

    for h, (member, part) in enumerate(heads):
        if part.start == 0:
            q = (nn(queries, proj(member, 0)) * scale).astype(bf16)
        qp_ref[h * count : (h + 1) * count, :] = (
            nt(q[:, part], proj(member, 1)[:, part]) * HD ** (-0.5)
        ).astype(bf16)

    def score(block, top):
        keys = x_ref[pl.ds(pl.multiple_of(block * KEYS, KEYS), KEYS), :]
        if not packed:
            energy = (nt(gram_high, keys) + nt(gram_low, keys)) * nt(eye, keys)
            scale = lax.rsqrt(jnp.sum(energy, axis=0, keepdims=True) / D + EPS)
            sc_ref[block] = jnp.broadcast_to(scale, (8, KEYS))
        scores = nt(qp_ref[...], keys) * sc_ref[block][:1]
        s_ref[block] = scores
        for part in range(KEYS // 128):
            top = jnp.maximum(top, scores[:, part * 128 : (part + 1) * 128])
        return top

    top = lax.fori_loop(0, TOKENS // KEYS, score, jnp.full((rows, 128), -1e30, f32))
    top = jnp.max(top, axis=1, keepdims=True)

    def mix(block, carry):
        total, mixed = carry
        expo = jnp.exp(s_ref[block] - top)
        for part in range(KEYS // 128):
            total = total + expo[:, part * 128 : (part + 1) * 128]
        weights = (expo * sc_ref[block][:1]).astype(bf16)
        keys = x_ref[pl.ds(pl.multiple_of(block * KEYS, KEYS), KEYS), :]
        return total, mixed + nn(weights, keys)

    total, mixed = lax.fori_loop(
        0, TOKENS // KEYS, mix, (jnp.zeros((rows, 128), f32), jnp.zeros((rows, BASIS), f32))
    )
    mixed = (mixed / jnp.sum(total, axis=1, keepdims=True)).astype(bf16)
    for load in loads:
        load.wait()
    values = [
        nn(mixed[h * count : (h + 1) * count], proj(member, 2)[:, part]) for h, (member, part) in enumerate(heads)
    ]
    values = jnp.concatenate(values, axis=1).astype(bf16)
    term = []
    for part in range(4):
        at = slice(part * QUART, (part + 1) * QUART)
        term.append(nt(values, jnp.concatenate([wout_ref[m, at, :] for m in range(members)], axis=1)))
    for d in range(DESTS):
        out_ref[d] = jnp.concatenate([t[d * OWN : (d + 1) * OWN] for t in term], axis=0).astype(bf16)


def attend(place, base, z, gram, proj, wout_at, wout):
    packed = z is not None
    members = 4 if packed else 2
    args = (base, z) if packed else (base,)
    rows = 2 * members * DESTS * OWN
    whole = lambda a: pl.BlockSpec(a.shape, lambda i: (0,) * a.ndim)
    out = jax.ShapeDtypeStruct((DESTS, 4 * OWN, QUART), bf16)
    return pl.pallas_call(
        lambda *refs: attend_kernel(members, packed, wout_at, *refs),
        out_shape=out,
        grid=(1,),
        in_specs=[pl.BlockSpec(memory_space=pltpu.SMEM)]
        + [whole(a) for a in (*args, gram, *proj)]
        + [pl.BlockSpec(memory_space=pl.ANY)],
        out_specs=whole(out),
        scratch_shapes=[
            pltpu.VMEM((TOKENS, BASIS), bf16),
            pltpu.VMEM((rows, BASIS), bf16),
            pltpu.VMEM((TOKENS // KEYS, rows, KEYS), f32),
            pltpu.VMEM((TOKENS // KEYS, 8, KEYS), f32),
            pltpu.VMEM((members, D, 128), bf16),
            pltpu.VMEM((N_SEC * N_TP * 8, 128), f32),
            pltpu.SemaphoreType.DMA((members,)),
        ],
        compiler_params=pltpu.CompilerParams(vmem_limit_bytes=VMEM),
        cost_estimate=pl.CostEstimate(flops=members * 2 * 10**9, bytes_accessed=10**7, transcendentals=rows * TOKENS),
        name="attend",
    )(place, *args, gram, *proj, wout)


def finish(recv_ref, senders, hidden, w_final):
    terms = recv_ref[senders[0]].astype(f32)
    for d in senders[1:]:
        terms = terms + recv_ref[d].astype(f32)
    afters = []
    energy = jnp.zeros((OWN, 1), f32)
    for part in range(4):
        after = hidden[:, part * QUART : (part + 1) * QUART] + terms[part * OWN : (part + 1) * OWN]
        energy = energy + jnp.sum(after * after, axis=1, keepdims=True)
        afters.append(after)
    scale = lax.rsqrt(energy / D + EPS)
    normed = jnp.concatenate([after * scale for after in afters], axis=1).astype(bf16)
    return nt(normed, w_final[...])


def own_kernel(place_ref, message_ref, high_ref, low_ref, x12_ref, hidden_ref):
    z, rest, hot = features(message_ref[...])
    lane = lax.broadcasted_iota(jnp.int32, z.shape, 1)
    full = jnp.concatenate([jnp.where(lane < CH, z, rest), hot], axis=1)
    x12 = nn(own_tokens(place_ref[1]).astype(bf16), full).astype(bf16)
    x12_ref[...] = x12
    hidden_ref[...] = nn(x12, high_ref[0]) + nn(x12, low_ref[0])


def scores_own_kernel(after_ref, x12_ref, high_ref, low_ref, hidden_ref):
    for net in range(2):
        hidden_ref[net] = nn(x12_ref[...], high_ref[net]) + nn(x12_ref[...], low_ref[net])


def student_kernel(
    place_ref, time_ref, recv_ref, hidden_ref, own12_ref, noise_ref, renoise_ref, wf_ref, gram_ref,
    x0_ref, noisy_ref, x12_ref, send_ref,
):
    pick = own_tokens(place_ref[1])
    x12 = own12_ref[...]
    velocity = finish(recv_ref, range(DESTS), hidden_ref[...], wf_ref)
    exact = lax.Precision.HIGHEST
    noise = jnp.dot(pick, noise_ref[...], precision=exact, preferred_element_type=f32)
    renoise = jnp.dot(pick, renoise_ref[...], precision=exact, preferred_element_type=f32)
    x0 = noise - velocity
    t = time_ref[0]
    noisy = (1.0 - t) * x0 + t * renoise
    x12 = jnp.concatenate([noisy.astype(bf16), x12[:, CH:]], axis=1)
    x0_ref[...] = x0
    noisy_ref[...] = noisy
    x12_ref[...] = x12
    row = lax.broadcasted_iota(jnp.int32, (OWN, 128), 0)
    lane = lax.broadcasted_iota(jnp.int32, (OWN, 128), 1)
    scales = jnp.zeros((OWN, 128), f32)
    for net in range(2):
        high, low = split2(gram_ref[net])
        energy = jnp.sum((nn(x12, high) + nn(x12, low)) * x12.astype(f32), axis=1, keepdims=True)
        for part, value in enumerate(split2(lax.rsqrt(energy / D + EPS))):
            scales = jnp.where(lane == row + (net * 32 + part * 16), value.astype(f32), scales)
    scales = jnp.sum(scales, axis=0, keepdims=True)
    pairs = [jnp.concatenate([noisy[j : j + 1], noisy[j + 1 : j + 2]], axis=1) for j in range(0, OWN, 2)]
    send_ref[...] = jnp.concatenate(pairs + [scales, jnp.zeros((1, 128), f32)], axis=0).astype(bf16)


def score_kernel(
    time_ref, recv_ref, x0_ref, noisy_ref, hidden_ref, wr_ref, wf_ref, send_ref
):
    noisy = noisy_ref[...]
    real = finish(recv_ref, range(4), hidden_ref[0], wr_ref)
    fake = finish(recv_ref, range(4, DESTS), hidden_ref[1], wf_ref)
    t = time_ref[0]
    gap = jnp.abs(x0_ref[...] - (noisy - t * real))
    gap = jnp.sum(jnp.sum(gap, axis=1, keepdims=True), axis=0, keepdims=True)
    grad = t * (real - fake)
    packed = [jnp.concatenate([grad[j : j + 1], grad[j + 1 : j + 2]], axis=1) for j in range(0, OWN, 2)]
    packed = jnp.concatenate([*packed, jnp.broadcast_to(gap, (1, 128)), jnp.zeros((1, 128), f32)], axis=0)
    send_ref[...] = jnp.broadcast_to(packed[None], send_ref.shape)


def call(kernel, shapes, smem, *args):
    def spec(arg):
        if isinstance(arg, tuple):
            array, n, at = arg
            return pl.BlockSpec((n, *array.shape[1:]), lambda i: (at,) + (0,) * (array.ndim - 1))
        return pl.BlockSpec(arg.shape, lambda i: (0,) * len(arg.shape))

    return pl.pallas_call(
        kernel,
        out_shape=shapes,
        grid=(1,),
        in_specs=[pl.BlockSpec(memory_space=pltpu.SMEM)] * smem + [spec(arg) for arg in args[smem:]],
        out_specs=jax.tree.map(spec, shapes),
        compiler_params=pltpu.CompilerParams(vmem_limit_bytes=VMEM),
        cost_estimate=pl.CostEstimate(flops=10**9, bytes_accessed=10**7, transcendentals=0),
        name=kernel.__name__,
    )(*[arg[0] if isinstance(arg, tuple) else arg for arg in args])


def swap(values, axes):
    return lax.all_to_all(values, axes, 0, 0, tiled=False)


def spread_to(values, axes, count):
    return swap(jnp.broadcast_to(values[None], (count, *values.shape)), axes)


def shift(values, axis, count, step):
    return lax.ppermute(values, axis, [((i + step) % count, i) for i in range(count)])


def place_tables():
    quarter = D // 4
    frequency = np.exp(-math.log(10000.0) * np.arange(quarter, dtype=np.float64) / quarter)
    table = np.zeros((GRID_H + GRID_W, D), np.float32)
    row = np.arange(GRID_H)[:, None] * frequency[None, :]
    col = np.arange(GRID_W)[:, None] * frequency[None, :]
    table[:GRID_H, : D // 2] = np.concatenate([np.sin(row), np.cos(row)], axis=1)
    table[GRID_H:, D // 2 :] = np.concatenate([np.sin(col), np.cos(col)], axis=1)
    high = table.astype(bf16)
    return jnp.asarray(high), jnp.asarray((table - high.astype(np.float32)).astype(bf16))


def time_embed(step_time):
    half_width = D // 2
    frequency = jnp.exp(-math.log(10000.0) * jnp.arange(half_width, dtype=f32) / half_width)
    angles = 1000.0 * step_time * frequency
    return jnp.concatenate([jnp.cos(angles), jnp.sin(angles)])


def per_device(
    student_noise,
    renoise_noise,
    patch_slot,
    renoise_step,
    prompt_ids,
    text_table,
    student_in,
    student_qkv,
    student_out,
    student_final,
    real_in,
    real_qkv,
    real_out,
    real_final,
    fake_in,
    fake_qkv,
    fake_out,
    fake_final,
):
    s = lax.axis_index(SEC)
    g = lax.axis_index(TP)
    core = lax.axis_index("core").astype(jnp.int32)
    place = jnp.stack([s, g, lax.axis_index("xl"), lax.axis_index("zh"), core]).astype(jnp.int32)
    step_time = renoise_step[0].astype(f32) / 1000.0

    vocab_local = text_table.shape[0]
    first_row = (s * N_TP + g) * vocab_local
    prompt_row = prompt_ids[0] - first_row
    matches = (prompt_row[:, None] == jnp.arange(vocab_local, dtype=jnp.int32)[None, :]).astype(f32)
    counts = jnp.sum(matches, axis=0).astype(bf16)
    partial_pool = nn(counts[None], text_table).reshape(D // 128, 128)
    noise = student_noise[0]
    packed = noise.astype(bf16)
    packed = jnp.concatenate([packed[:SLOTS], packed[SLOTS:]], axis=1)
    slot = patch_slot[0]
    lines = jnp.stack([slot // GRID_W, slot % GRID_W]).astype(bf16)
    lines = jnp.pad(jnp.pad(lines, ((0, 0), (0, 64))).reshape(4, 128), ((0, 4), (0, 0)))
    own = jnp.concatenate([packed, lines, *split2(partial_pool), jnp.zeros((2, 128), bf16)], axis=0)
    out_peer = shift(student_out, "xl", 2, 1)[None]
    out_peer, own = lax.optimization_barrier((out_peer, own))
    base = spread_to(own, SEC, N_SEC)
    out2 = jnp.stack([real_out, fake_out])
    out2, own = lax.optimization_barrier((out2, own))
    out2 = lax.all_gather(out2, "zh", axis=0, tiled=True)
    shares = base[:, SHARES : SHARES + 38].astype(f32).reshape(N_SEC * 2, D // 128, 128)
    shares = jnp.sum(shares, axis=0)
    shares, out2 = lax.optimization_barrier((shares, out2))
    shares = spread_to(shares, TP, N_TP)

    def columns(qkv):
        return jnp.transpose(qkv, (1, 0, 2))

    def gather(*parts):
        return lax.all_gather(jnp.concatenate(parts, axis=0), SEC, axis=1, tiled=True)

    first = gather(columns(student_qkv), student_out[None], out_peer)

    one = jax.ShapeDtypeStruct
    tables = place_tables()

    def prepare(shares, times, *w_in):
        n = len(w_in)
        shapes = (one((n, BASIS, D), bf16), one((n, BASIS, D), bf16), one((n, BASIS, BASIS), f32))
        return call(prepare_kernel, shapes, 0, *tables, jnp.stack([time_embed(t) for t in times]), shares, *w_in)

    def pack(qkv, net):
        return jnp.concatenate([columns(qkv), out2.reshape(4, 2, *student_out.shape)[:, net]], axis=0)

    both = (pack(real_qkv, 0), pack(fake_qkv, 1))
    mine = jnp.where(core == 0, both[0], both[1])
    peer = jnp.where(core == 0, both[1], both[0])
    peer, mine, shares = lax.optimization_barrier((peer, mine, shares))
    peer = shift(peer, "core", 2, 1)
    second = jnp.concatenate([jnp.where(core == 0, mine, peer), jnp.where(core == 0, peer, mine)], axis=1)
    high1, low1, gram1 = prepare(shares, (jnp.float32(1.0),), student_in)
    first, gram1 = lax.optimization_barrier((first, gram1))
    second, first = lax.optimization_barrier((second, first))
    second = lax.all_gather(second, "y", axis=1, tiled=True)
    proj1 = project(jnp.zeros((2,), jnp.int32), high1, first)
    peer1 = shift(proj1, "xl", 2, 1)
    place, proj1 = lax.optimization_barrier((place, proj1))
    x12, hidden = call(
        own_kernel, (one((OWN, BASIS), bf16), one((OWN, D), f32)), 1, place, own, (high1, 1, 0), (low1, 1, 0)
    )
    place, hidden = lax.optimization_barrier((place, hidden))
    terms = attend(place, base, None, gram1, (proj1, peer1), 3, first)
    shares, terms = lax.optimization_barrier((shares, terms))
    high, low, gram = prepare(shares, (step_time, step_time), real_in, fake_in)
    terms = swap(terms, ("zh", "zp"))
    terms, gram = lax.optimization_barrier((terms, gram))
    x0, noisy, x12, message = call(
        student_kernel,
        (one((OWN, CH), f32), one((OWN, CH), f32), one((OWN, BASIS), bf16), one((8, 128), bf16)),
        2,
        place,
        step_time[None],
        terms,
        hidden,
        x12,
        noise,
        renoise_noise[0],
        student_final.T,
        (gram, 2, 0),
    )
    near = spread_to(message, TP, N_TP).reshape(N_TP * 8, 128)
    pick, second, unused = lax.optimization_barrier((jnp.stack([core, core * 0]), second, message))
    proj2 = project(pick, high, second)
    proj2 = lax.all_gather(proj2, "zh", axis=0, tiled=False)
    everyone = spread_to(near, SEC, N_SEC).reshape(N_SEC * N_TP * 8, 128)
    terms = attend(place, base, everyone, gram, (proj2,), 3, second)
    x12, terms = lax.optimization_barrier((x12, terms))
    hidden = call(
        scores_own_kernel, one((2, OWN, D), f32), 1, place, x12, (high, 2, 0), (low, 2, 0)
    )
    terms = swap(terms, ("core", "xl", "zp"))
    message = call(
        score_kernel,
        one((N_TP, 8, 128), f32),
        1,
        step_time[None],
        terms,
        x0,
        noisy,
        hidden,
        real_final.T,
        fake_final.T,
    )
    near = swap(message, TP)
    gap = spread_to(jnp.sum(near[:, 6:7], axis=0), SEC, N_SEC)
    spread = jnp.sum(gap[:, 0, 0]) / (TOKENS * CH) + 1e-05
    grad = jnp.transpose(near[:, :6].reshape(N_TP, 6, 2, CH), (1, 2, 0, 3))
    return (grad.reshape(LOCAL, CH) / spread)[None]


def solution(mesh):
    fine = Mesh(mesh.devices.reshape(8, 2, 2, 4, 2, 2), ("y", "core", "xl", "zh", "zp", "rep"))
    qkv = P(SEC, None, TP)
    out = P(SEC, TP)
    net = (P(), qkv, out, P())
    placed = (
        P("rep", SEC, None),
        P("rep", SEC, None),
        P("rep", SEC),
        P("rep"),
        P("rep", None),
        P(SEC + TP, None),
    ) + net * 3
    return jax.shard_map(
        per_device, mesh=fine, in_specs=placed, out_specs=P("rep", SEC, None), check_vma=False
    )
```

```python
import math

import jax
import jax.numpy as jnp
import numpy as np
from jax import lax
from jax.experimental import pallas as pl
from jax.experimental.pallas import tpu as pltpu
from jax.sharding import Mesh, PartitionSpec as P

D = 2432
HD = 64
GRID_W = 64
GRID_H = 48
CH = 64
BASIS = 192
ROW0, ONE, COL0 = 64, 112, 128
EPS = 1e-06
SEC = ("y", "core")
TP = ("xl", "zh", "zp")
N_SEC = 16
PROMPT = 256
N_TP = 16
LOCAL = 192
OWN = 12
DESTS = 8
TOKENS = 3072
KEYS = 1536
QUART = D // 4
SLOTS, SHARES, MESSAGE = 96, 104, 144
VMEM = 60 * 2**20
bf16 = jnp.bfloat16
f32 = jnp.float32


def nn(a, b):
    return jnp.dot(a, b, preferred_element_type=f32)


def nt(a, b):
    return lax.dot_general(a, b, (((1,), (1,)), ((), ())), preferred_element_type=f32)


def split2(values):
    high = values.astype(bf16)
    return high, (values - high.astype(f32)).astype(bf16)


def features(message):
    z = message[:SLOTS]
    z = jnp.concatenate([z, jnp.concatenate([z[:, CH:], z[:, :CH]], axis=1)], axis=0)
    slots = message[SLOTS:SHARES].astype(f32).T
    row = jnp.concatenate([slots[:, 0:1], slots[:64, 1:2]], axis=0)
    col = jnp.concatenate([slots[:, 2:3], slots[:64, 3:4]], axis=0)
    lane = lax.broadcasted_iota(jnp.int32, (LOCAL, 128), 1).astype(f32)
    rest = ((lane == row + ROW0) | (lane == ONE)).astype(f32).astype(bf16)
    hot = (lane[:, :GRID_W] == col).astype(f32).astype(bf16)
    return z, rest, hot


def own_tokens(g):
    row = lax.broadcasted_iota(jnp.int32, (OWN, LOCAL), 0)
    col = lax.broadcasted_iota(jnp.int32, (OWN, LOCAL), 1)
    return (col == row * N_TP + g).astype(f32)


def prepare_kernel(high_ref, low_ref, time_ref, shares_ref, *refs):
    *w_refs, hid_high_ref, hid_low_ref, gram_ref = refs
    pooled = shares_ref[0]
    for g in range(1, N_TP):
        pooled = pooled + shares_ref[g]
    pooled = pooled / PROMPT
    pooled = jnp.concatenate([pooled[k : k + 1] for k in range(D // 128)], axis=1)
    is_one = lax.broadcasted_iota(jnp.int32, (16, D), 0) == 0
    for net, w_ref in enumerate(w_refs):
        bias = jnp.broadcast_to(time_ref[net : net + 1, :] + pooled, (16, D))
        bias = jnp.where(is_one, bias, 0.0)
        for ref, table_ref, part in zip((hid_high_ref, hid_low_ref), (high_ref, low_ref), split2(bias)):
            ref[net, :CH, :] = w_ref[...] if ref is hid_high_ref else jnp.zeros((CH, D), bf16)
            ref[net, ROW0:ONE, :] = table_ref[:GRID_H]
            ref[net, ONE:COL0, :] = part
            ref[net, COL0:, :] = table_ref[GRID_H:]
        high, low = hid_high_ref[net], hid_low_ref[net]
        cross = nt(high, low)
        gram_ref[net] = nt(high, high) + cross + nt(low, high)


def project_kernel(pick_ref, hid_ref, w_ref, out_ref):
    out = nn(hid_ref[0], jnp.concatenate([w_ref[k] for k in range(3)], axis=1)).astype(bf16)
    for k in range(3):
        out_ref[k] = out[:, k * 128 : (k + 1) * 128]


def project(pick, hid, w):
    return pl.pallas_call(
        project_kernel,
        grid_spec=pltpu.PrefetchScalarGridSpec(
            num_scalar_prefetch=1,
            grid=(1,),
            in_specs=[
                pl.BlockSpec((1, BASIS, D), lambda i, pick: (pick[0], 0, 0)),
                pl.BlockSpec((3, D, 128), lambda i, pick: (pick[1], 0, 0)),
            ],
            out_specs=pl.BlockSpec((3, BASIS, 128), lambda i, pick: (0, 0, 0)),
        ),
        out_shape=jax.ShapeDtypeStruct((3, BASIS, 128), bf16),
        compiler_params=pltpu.CompilerParams(vmem_limit_bytes=VMEM),
        cost_estimate=pl.CostEstimate(flops=2 * BASIS * D * 384, bytes_accessed=3 * 10**6, transcendentals=0),
        name="project",
    )(pick, hid, w)


def attend_kernel(members, packed, wout_at, place_ref, base_ref, *refs):
    if packed:
        z_ref, *refs = refs
    gram_ref, *refs = refs
    proj_refs = refs[:-9]
    wout_hbm, out_ref, x_ref, qp_ref, s_ref, sc_ref, wout_ref, z32_ref, sem = refs[-9:]
    s, xl, zh, core = place_ref[0], place_ref[2], place_ref[3], place_ref[4]
    count = DESTS * OWN
    net = core if packed else 0
    loads = [
        pltpu.make_async_copy(wout_hbm.at[wout_at + m], wout_ref.at[m], sem.at[m])
        for m in range(members)
    ]
    for load in loads:
        load.start()
    if packed:
        z32_ref[...] = z_ref[...].astype(f32)
        for sec in range(N_SEC):
            unused, rest, hot = features(base_ref[sec])
            for j in range(OWN):
                at = (j * N_SEC + sec) * 16
                x_ref[at : at + 16, :128] = rest[j * 16 : (j + 1) * 16]
                x_ref[at : at + 16, COL0:] = hot[j * 16 : (j + 1) * 16]
        lane = lax.broadcasted_iota(jnp.int32, (256, 128), 1)
        for j in range(OWN):
            chunk = z32_ref[pl.ds(j // 2, 256, stride=8), :].astype(bf16)
            if j % 2:
                chunk = jnp.concatenate([chunk[:, 64:], chunk[:, :64]], axis=1)
            at = slice(j * 256, (j + 1) * 256)
            x_ref[at, :128] = jnp.where(lane < CH, chunk, x_ref[at, :128])
        own = jnp.concatenate(
            [
                x_ref[pl.ds(pl.multiple_of((j * N_SEC + s - core + other) * 16, 16), 16), :]
                for other in range(2)
                for j in range(OWN)
            ],
            axis=0,
        )
        scales = z32_ref[pl.ds(6, 256, stride=8), :].T
        scales = jnp.where(core == 0, scales[:32], scales[32:64])
        for j in range(OWN):
            line = scales[j : j + 1] + scales[j + 16 : j + 17]
            at = j * 256
            sc_ref[at // KEYS, :, at % KEYS : at % KEYS + 256] = jnp.broadcast_to(line, (8, 256))
    else:
        for sec in range(N_SEC):
            z, rest, hot = features(base_ref[sec])
            lane = lax.broadcasted_iota(jnp.int32, z.shape, 1)
            x_ref[sec * LOCAL : (sec + 1) * LOCAL, :128] = jnp.where(lane < CH, z, rest)
            x_ref[sec * LOCAL : (sec + 1) * LOCAL, COL0:] = hot
        own = x_ref[pl.ds(pl.multiple_of(s * LOCAL, LOCAL), LOCAL), :]
    row = lax.broadcasted_iota(jnp.int32, (count, own.shape[0]), 0)
    col = lax.broadcasted_iota(jnp.int32, (count, own.shape[0]), 1)
    share = lax.shift_right_logical(row * 171, 11)
    token = row - share * OWN
    if packed:
        half = lax.shift_right_logical(share, 2)
        owner = lax.bitwise_and(lax.shift_right_logical(share, 1), 1) * 8 + zh * 2 + lax.bitwise_and(share, 1)
        order = (col == half * LOCAL + token * N_TP + owner).astype(bf16)
    else:
        order = (col == token * N_TP + xl * 8 + share).astype(bf16)
    queries = nn(order, own).astype(bf16)
    eye = (
        lax.broadcasted_iota(jnp.int32, (BASIS, BASIS), 0) == lax.broadcasted_iota(jnp.int32, (BASIS, BASIS), 1)
    ).astype(bf16)
    heads = [(member, slice(half * HD, (half + 1) * HD)) for member in range(members) for half in range(2)]
    rows = len(heads) * count
    gram_high, gram_low = split2(gram_ref[net])
    energy = jnp.sum(
        (nn(queries, gram_high) + nn(queries, gram_low)) * queries.astype(f32), axis=1, keepdims=True
    )
    scale = lax.rsqrt(energy / D + EPS)

    def proj(member, kind):
        return proj_refs[0][member, kind] if packed else proj_refs[member][kind]

    for h, (member, part) in enumerate(heads):
        if part.start == 0:
            q = (nn(queries, proj(member, 0)) * scale).astype(bf16)
        qp_ref[h * count : (h + 1) * count, :] = (
            nt(q[:, part], proj(member, 1)[:, part]) * HD ** (-0.5)
        ).astype(bf16)

    def score(block, top):
        keys = x_ref[pl.ds(pl.multiple_of(block * KEYS, KEYS), KEYS), :]
        if not packed:
            energy = (nt(gram_high, keys) + nt(gram_low, keys)) * nt(eye, keys)
            scale = lax.rsqrt(jnp.sum(energy, axis=0, keepdims=True) / D + EPS)
            sc_ref[block] = jnp.broadcast_to(scale, (8, KEYS))
        scores = nt(qp_ref[...], keys) * sc_ref[block][:1]
        s_ref[block] = scores
        for part in range(KEYS // 128):
            top = jnp.maximum(top, scores[:, part * 128 : (part + 1) * 128])
        return top

    top = lax.fori_loop(0, TOKENS // KEYS, score, jnp.full((rows, 128), -1e30, f32))
    top = jnp.max(top, axis=1, keepdims=True)

    def mix(block, carry):
        total, mixed = carry
        expo = jnp.exp(s_ref[block] - top)
        for part in range(KEYS // 128):
            total = total + expo[:, part * 128 : (part + 1) * 128]
        weights = (expo * sc_ref[block][:1]).astype(bf16)
        keys = x_ref[pl.ds(pl.multiple_of(block * KEYS, KEYS), KEYS), :]
        return total, mixed + nn(weights, keys)

    total, mixed = lax.fori_loop(
        0, TOKENS // KEYS, mix, (jnp.zeros((rows, 128), f32), jnp.zeros((rows, BASIS), f32))
    )
    mixed = (mixed / jnp.sum(total, axis=1, keepdims=True)).astype(bf16)
    for load in loads:
        load.wait()
    values = [
        nn(mixed[h * count : (h + 1) * count], proj(member, 2)[:, part]) for h, (member, part) in enumerate(heads)
    ]
    values = jnp.concatenate(values, axis=1).astype(bf16)
    term = []
    for part in range(4):
        at = slice(part * QUART, (part + 1) * QUART)
        term.append(nt(values, jnp.concatenate([wout_ref[m, at, :] for m in range(members)], axis=1)))
    for d in range(DESTS):
        out_ref[d] = jnp.concatenate([t[d * OWN : (d + 1) * OWN] for t in term], axis=0).astype(bf16)


def attend(place, base, z, gram, proj, wout_at, wout):
    packed = z is not None
    members = 4 if packed else 2
    args = (base, z) if packed else (base,)
    rows = 2 * members * DESTS * OWN
    whole = lambda a: pl.BlockSpec(a.shape, lambda i: (0,) * a.ndim)
    out = jax.ShapeDtypeStruct((DESTS, 4 * OWN, QUART), bf16)
    return pl.pallas_call(
        lambda *refs: attend_kernel(members, packed, wout_at, *refs),
        out_shape=out,
        grid=(1,),
        in_specs=[pl.BlockSpec(memory_space=pltpu.SMEM)]
        + [whole(a) for a in (*args, gram, *proj)]
        + [pl.BlockSpec(memory_space=pl.ANY)],
        out_specs=whole(out),
        scratch_shapes=[
            pltpu.VMEM((TOKENS, BASIS), bf16),
            pltpu.VMEM((rows, BASIS), bf16),
            pltpu.VMEM((TOKENS // KEYS, rows, KEYS), f32),
            pltpu.VMEM((TOKENS // KEYS, 8, KEYS), f32),
            pltpu.VMEM((members, D, 128), bf16),
            pltpu.VMEM((N_SEC * N_TP * 8, 128), f32),
            pltpu.SemaphoreType.DMA((members,)),
        ],
        compiler_params=pltpu.CompilerParams(vmem_limit_bytes=VMEM),
        cost_estimate=pl.CostEstimate(flops=members * 2 * 10**9, bytes_accessed=10**7, transcendentals=rows * TOKENS),
        name="attend",
    )(place, *args, gram, *proj, wout)


def finish(recv_ref, senders, hidden, w_final):
    terms = recv_ref[senders[0]].astype(f32)
    for d in senders[1:]:
        terms = terms + recv_ref[d].astype(f32)
    afters = []
    energy = jnp.zeros((OWN, 1), f32)
    for part in range(4):
        after = hidden[:, part * QUART : (part + 1) * QUART] + terms[part * OWN : (part + 1) * OWN]
        energy = energy + jnp.sum(after * after, axis=1, keepdims=True)
        afters.append(after)
    scale = lax.rsqrt(energy / D + EPS)
    normed = jnp.concatenate([after * scale for after in afters], axis=1).astype(bf16)
    return nt(normed, w_final[...])


def own_kernel(place_ref, message_ref, high_ref, low_ref, x12_ref, hidden_ref):
    z, rest, hot = features(message_ref[...])
    lane = lax.broadcasted_iota(jnp.int32, z.shape, 1)
    full = jnp.concatenate([jnp.where(lane < CH, z, rest), hot], axis=1)
    x12 = nn(own_tokens(place_ref[1]).astype(bf16), full).astype(bf16)
    x12_ref[...] = x12
    hidden_ref[...] = nn(x12, high_ref[0]) + nn(x12, low_ref[0])


def scores_own_kernel(after_ref, x12_ref, high_ref, low_ref, hidden_ref):
    for net in range(2):
        hidden_ref[net] = nn(x12_ref[...], high_ref[net]) + nn(x12_ref[...], low_ref[net])


def student_kernel(
    place_ref, time_ref, recv_ref, hidden_ref, own12_ref, noise_ref, renoise_ref, wf_ref, gram_ref,
    x0_ref, noisy_ref, x12_ref, send_ref,
):
    pick = own_tokens(place_ref[1])
    x12 = own12_ref[...]
    velocity = finish(recv_ref, range(DESTS), hidden_ref[...], wf_ref)
    exact = lax.Precision.HIGHEST
    noise = jnp.dot(pick, noise_ref[...], precision=exact, preferred_element_type=f32)
    renoise = jnp.dot(pick, renoise_ref[...], precision=exact, preferred_element_type=f32)
    x0 = noise - velocity
    t = time_ref[0]
    noisy = (1.0 - t) * x0 + t * renoise
    x12 = jnp.concatenate([noisy.astype(bf16), x12[:, CH:]], axis=1)
    x0_ref[...] = x0
    noisy_ref[...] = noisy
    x12_ref[...] = x12
    row = lax.broadcasted_iota(jnp.int32, (OWN, 128), 0)
    lane = lax.broadcasted_iota(jnp.int32, (OWN, 128), 1)
    scales = jnp.zeros((OWN, 128), f32)
    for net in range(2):
        high, low = split2(gram_ref[net])
        energy = jnp.sum((nn(x12, high) + nn(x12, low)) * x12.astype(f32), axis=1, keepdims=True)
        for part, value in enumerate(split2(lax.rsqrt(energy / D + EPS))):
            scales = jnp.where(lane == row + (net * 32 + part * 16), value.astype(f32), scales)
    scales = jnp.sum(scales, axis=0, keepdims=True)
    pairs = [jnp.concatenate([noisy[j : j + 1], noisy[j + 1 : j + 2]], axis=1) for j in range(0, OWN, 2)]
    send_ref[...] = jnp.concatenate(pairs + [scales, jnp.zeros((1, 128), f32)], axis=0).astype(bf16)


def score_kernel(
    time_ref, recv_ref, x0_ref, noisy_ref, hidden_ref, wr_ref, wf_ref, send_ref
):
    noisy = noisy_ref[...]
    real = finish(recv_ref, range(4), hidden_ref[0], wr_ref)
    fake = finish(recv_ref, range(4, DESTS), hidden_ref[1], wf_ref)
    t = time_ref[0]
    gap = jnp.abs(x0_ref[...] - (noisy - t * real))
    gap = jnp.sum(jnp.sum(gap, axis=1, keepdims=True), axis=0, keepdims=True)
    grad = t * (real - fake)
    packed = [jnp.concatenate([grad[j : j + 1], grad[j + 1 : j + 2]], axis=1) for j in range(0, OWN, 2)]
    packed = jnp.concatenate([*packed, jnp.broadcast_to(gap, (1, 128)), jnp.zeros((1, 128), f32)], axis=0)
    send_ref[...] = jnp.broadcast_to(packed[None], send_ref.shape)


def call(kernel, shapes, smem, *args):
    def spec(arg):
        if isinstance(arg, tuple):
            array, n, at = arg
            return pl.BlockSpec((n, *array.shape[1:]), lambda i: (at,) + (0,) * (array.ndim - 1))
        return pl.BlockSpec(arg.shape, lambda i: (0,) * len(arg.shape))

    return pl.pallas_call(
        kernel,
        out_shape=shapes,
        grid=(1,),
        in_specs=[pl.BlockSpec(memory_space=pltpu.SMEM)] * smem + [spec(arg) for arg in args[smem:]],
        out_specs=jax.tree.map(spec, shapes),
        compiler_params=pltpu.CompilerParams(vmem_limit_bytes=VMEM),
        cost_estimate=pl.CostEstimate(flops=10**9, bytes_accessed=10**7, transcendentals=0),
        name=kernel.__name__,
    )(*[arg[0] if isinstance(arg, tuple) else arg for arg in args])


def swap(values, axes):
    return lax.all_to_all(values, axes, 0, 0, tiled=False)


def spread_to(values, axes, count):
    return swap(jnp.broadcast_to(values[None], (count, *values.shape)), axes)


def shift(values, axis, count, step):
    return lax.ppermute(values, axis, [((i + step) % count, i) for i in range(count)])


def place_tables():
    quarter = D // 4
    frequency = np.exp(-math.log(10000.0) * np.arange(quarter, dtype=np.float64) / quarter)
    table = np.zeros((GRID_H + GRID_W, D), np.float32)
    row = np.arange(GRID_H)[:, None] * frequency[None, :]
    col = np.arange(GRID_W)[:, None] * frequency[None, :]
    table[:GRID_H, : D // 2] = np.concatenate([np.sin(row), np.cos(row)], axis=1)
    table[GRID_H:, D // 2 :] = np.concatenate([np.sin(col), np.cos(col)], axis=1)
    high = table.astype(bf16)
    return jnp.asarray(high), jnp.asarray((table - high.astype(np.float32)).astype(bf16))


def time_embed(step_time):
    half_width = D // 2
    frequency = jnp.exp(-math.log(10000.0) * jnp.arange(half_width, dtype=f32) / half_width)
    angles = 1000.0 * step_time * frequency
    return jnp.concatenate([jnp.cos(angles), jnp.sin(angles)])


def per_device(
    student_noise,
    renoise_noise,
    patch_slot,
    renoise_step,
    prompt_ids,
    text_table,
    student_in,
    student_qkv,
    student_out,
    student_final,
    real_in,
    real_qkv,
    real_out,
    real_final,
    fake_in,
    fake_qkv,
    fake_out,
    fake_final,
):
    s = lax.axis_index(SEC)
    g = lax.axis_index(TP)
    core = lax.axis_index("core").astype(jnp.int32)
    place = jnp.stack([s, g, lax.axis_index("xl"), lax.axis_index("zh"), core]).astype(jnp.int32)
    step_time = renoise_step[0].astype(f32) / 1000.0

    vocab_local = text_table.shape[0]
    first_row = (s * N_TP + g) * vocab_local
    prompt_row = prompt_ids[0] - first_row
    matches = (prompt_row[:, None] == jnp.arange(vocab_local, dtype=jnp.int32)[None, :]).astype(f32)
    counts = jnp.sum(matches, axis=0).astype(bf16)
    partial_pool = nn(counts[None], text_table).reshape(D // 128, 128)
    noise = student_noise[0]
    packed = noise.astype(bf16)
    packed = jnp.concatenate([packed[:SLOTS], packed[SLOTS:]], axis=1)
    slot = patch_slot[0]
    lines = jnp.stack([slot // GRID_W, slot % GRID_W]).astype(bf16)
    lines = jnp.pad(jnp.pad(lines, ((0, 0), (0, 64))).reshape(4, 128), ((0, 4), (0, 0)))
    own = jnp.concatenate([packed, lines, *split2(partial_pool), jnp.zeros((2, 128), bf16)], axis=0)
    out_peer = shift(student_out, "xl", 2, 1)[None]
    out_peer, own = lax.optimization_barrier((out_peer, own))
    base = spread_to(own, SEC, N_SEC)
    out2 = jnp.stack([real_out, fake_out])
    out2, own = lax.optimization_barrier((out2, own))
    out2 = lax.all_gather(out2, "zh", axis=0, tiled=True)
    shares = base[:, SHARES : SHARES + 38].astype(f32).reshape(N_SEC * 2, D // 128, 128)
    shares = jnp.sum(shares, axis=0)
    shares, out2 = lax.optimization_barrier((shares, out2))
    shares = spread_to(shares, TP, N_TP)

    def columns(qkv):
        return jnp.transpose(qkv, (1, 0, 2))

    def gather(*parts):
        return lax.all_gather(jnp.concatenate(parts, axis=0), SEC, axis=1, tiled=True)

    first = gather(columns(student_qkv), student_out[None], out_peer)

    one = jax.ShapeDtypeStruct
    tables = place_tables()

    def prepare(shares, times, *w_in):
        n = len(w_in)
        shapes = (one((n, BASIS, D), bf16), one((n, BASIS, D), bf16), one((n, BASIS, BASIS), f32))
        return call(prepare_kernel, shapes, 0, *tables, jnp.stack([time_embed(t) for t in times]), shares, *w_in)

    def pack(qkv, net):
        return jnp.concatenate([columns(qkv), out2.reshape(4, 2, *student_out.shape)[:, net]], axis=0)

    both = (pack(real_qkv, 0), pack(fake_qkv, 1))
    mine = jnp.where(core == 0, both[0], both[1])
    high1, low1, gram1 = prepare(shares, (jnp.float32(1.0),), student_in)
    first, gram1 = lax.optimization_barrier((first, gram1))
    proj1 = project(jnp.zeros((2,), jnp.int32), high1, first)
    peer1 = shift(proj1, "xl", 2, 1)
    place, proj1 = lax.optimization_barrier((place, proj1))
    x12, hidden = call(
        own_kernel, (one((OWN, BASIS), bf16), one((OWN, D), f32)), 1, place, own, (high1, 1, 0), (low1, 1, 0)
    )
    place, hidden = lax.optimization_barrier((place, hidden))
    peer = jnp.where(core == 0, both[1], both[0])
    peer, mine, hidden = lax.optimization_barrier((peer, mine, hidden))
    peer = shift(peer, "core", 2, 1)
    second = jnp.concatenate([jnp.where(core == 0, mine, peer), jnp.where(core == 0, peer, mine)], axis=1)
    second, first = lax.optimization_barrier((second, first))
    second = lax.all_gather(second, "y", axis=1, tiled=True)
    terms = attend(place, base, None, gram1, (proj1, peer1), 3, first)
    shares, terms = lax.optimization_barrier((shares, terms))
    high, low, gram = prepare(shares, (step_time, step_time), real_in, fake_in)
    terms = swap(terms, ("zh", "zp"))
    terms, gram = lax.optimization_barrier((terms, gram))
    x0, noisy, x12, message = call(
        student_kernel,
        (one((OWN, CH), f32), one((OWN, CH), f32), one((OWN, BASIS), bf16), one((8, 128), bf16)),
        2,
        place,
        step_time[None],
        terms,
        hidden,
        x12,
        noise,
        renoise_noise[0],
        student_final.T,
        (gram, 2, 0),
    )
    near = spread_to(message, TP, N_TP).reshape(N_TP * 8, 128)
    pick, second, unused = lax.optimization_barrier((jnp.stack([core, core * 0]), second, message))
    proj2 = project(pick, high, second)
    proj2 = lax.all_gather(proj2, "zh", axis=0, tiled=False)
    everyone = spread_to(near, SEC, N_SEC).reshape(N_SEC * N_TP * 8, 128)
    terms = attend(place, base, everyone, gram, (proj2,), 3, second)
    x12, terms = lax.optimization_barrier((x12, terms))
    hidden = call(
        scores_own_kernel, one((2, OWN, D), f32), 1, place, x12, (high, 2, 0), (low, 2, 0)
    )
    terms = swap(terms, ("core", "xl", "zp"))
    message = call(
        score_kernel,
        one((N_TP, 8, 128), f32),
        1,
        step_time[None],
        terms,
        x0,
        noisy,
        hidden,
        real_final.T,
        fake_final.T,
    )
    near = swap(message, TP)
    gap = spread_to(jnp.sum(near[:, 6:7], axis=0), SEC, N_SEC)
    spread = jnp.sum(gap[:, 0, 0]) / (TOKENS * CH) + 1e-05
    grad = jnp.transpose(near[:, :6].reshape(N_TP, 6, 2, CH), (1, 2, 0, 3))
    return (grad.reshape(LOCAL, CH) / spread)[None]


def solution(mesh):
    fine = Mesh(mesh.devices.reshape(8, 2, 2, 4, 2, 2), ("y", "core", "xl", "zh", "zp", "rep"))
    qkv = P(SEC, None, TP)
    out = P(SEC, TP)
    net = (P(), qkv, out, P())
    placed = (
        P("rep", SEC, None),
        P("rep", SEC, None),
        P("rep", SEC),
        P("rep"),
        P("rep", None),
        P(SEC + TP, None),
    ) + net * 3
    return jax.shard_map(
        per_device, mesh=fine, in_specs=placed, out_specs=P("rep", SEC, None), check_vma=False
    )
```
